256 devices in a mesh: token: 16 (over x_lo, y, core), brow: 8 (over z), bcol: 2 (over x_hi).
Axes of the slice: x: 4 (x_hi: 2, x_lo: 2; x = x_hi * 2 + x_lo), y: 4, z: 8, core: 2. Of those that a mesh axis runs over, the one named last changes fastest.
Arguments:
- layer_input: bfloat16 [16384, 8192], P('token', ('brow', 'bcol')), may hold values from -6 to 6
- pairs: int32 [2, 16, 32], P(None, ('brow', 'bcol')), may hold values from 0 to 31, as said below
- counts: int32 [16], P(('brow', 'bcol')), may hold values from 1 to 32, 320 in all
Outputs:
- hessian_blocks: float32 [16, 32, 256, 256], P(('brow', 'bcol'), 'token')
The draws below stay inside these ranges and needn't reach their ends.
Inputs may be any that keep to these rules, and one draw needn't show every extreme that they name: `pairs`: reader r's pair rows lie in block rows 4 * (r // 2) to 4 * (r // 2) + 3, and each pair's row and column differ by less than 4.
All inputs are finite; a program needn't handle non-finite values. No bound on the sum of `counts` on one device may be relied on, other than what follows from the above.
Results may differ from the reference program's by a relative error of at most 0.0003.
Values may be sent and summed in bfloat16 or wider, within the bound.
A program may use at most 128 MiB of HBM per device.

```python
import math
from functools import partial
import jax
import jax.numpy as jnp
import numpy as np
from jax import lax

D = 8192
BS = 256
BAND = 4
LB = 32
TOKENS = 16384
NB = 32
READERS = 16
RPB = 4
N_BCOL = 2


def draw_pairs(key, part):
    key = jax.random.fold_in(key, 11)
    key_rows, key_offset, key_sign = jax.random.split(key, 3)
    reader_ids = jnp.arange(READERS, dtype=jnp.int32)[:, None]
    band_index = reader_ids // N_BCOL
    row_blocks = band_index * RPB + jax.random.randint(key_rows, (READERS, LB), 0, RPB)
    offsets = jax.random.randint(key_offset, (READERS, LB), 0, BAND)
    signs = jax.random.randint(key_sign, (READERS, LB), 0, 2) * 2 - 1
    candidate = row_blocks + signs * offsets
    outside = (candidate < 0) | (candidate >= NB)
    col_blocks = jnp.where(outside, row_blocks - signs * offsets, candidate)
    row_blocks = row_blocks.at[0, 0].set(0)
    col_blocks = col_blocks.at[0, 0].set(0)
    row_blocks = row_blocks.at[READERS - 1, 0].set(NB - 1)
    col_blocks = col_blocks.at[READERS - 1, 0].set(NB - 1)
    return jnp.stack([row_blocks, col_blocks]).astype(jnp.int32)


def steps_of(own_key, extent, cuts, least, largest):
    level = 1.0
    for axis_at, shards_of in cuts:
        heights = jax.random.uniform(jax.random.fold_in(jax.random.fold_in(own_key, 6), axis_at), (shards_of,), jnp.float32, least / len(cuts), largest / len(cuts))
        level = level * jnp.repeat(jnp.exp(heights), extent[axis_at] // shards_of).reshape((-1,) + (1,) * (len(extent) - 1 - axis_at))
    return level


def length_profile(number_of, total, reach, skew):
    weights = [(1 << 20) // math.isqrt(standing ** skew) + 1 for standing in range(2, number_of + 1)]
    surplus, given = total - reach - (number_of - 1), [1] * (number_of - 1)
    while surplus > 0:
        free = [i for i in range(number_of - 1) if given[i] < reach]
        mass, remaining = sum([weights[i] for i in free]), surplus
        for i in free:
            extra = min(reach - given[i], max(1, remaining * weights[i] // mass), surplus)
            given[i] = given[i] + extra
            surplus = surplus - extra
    return np.array([reach] + given)


def ragged_sizes(rng, count, total, limit, slope):
    if count == 2:
        one = jax.random.randint(rng, (), max(1, total - limit), min(limit, total - 1) + 1)
        return jnp.stack([one, total - one])
    sizes = jnp.asarray(length_profile(count, total, limit, slope), jnp.int32)
    couples = (count - 1) // 2
    source_of, taker = sizes[1:1 + 2 * couples:2], sizes[2:2 + 2 * couples:2]
    slack = jnp.minimum(source_of - 1, limit - taker)
    passed = jax.random.randint(jax.random.fold_in(rng, 1), (couples,), 0, 1 << 20) % (slack + 1)
    sizes = sizes.at[1:1 + 2 * couples:2].set(source_of - passed).at[2:2 + 2 * couples:2].set(taker + passed)
    return sizes[jax.random.permutation(jax.random.fold_in(rng, 2), count)]


def centred(stream_key, extent, scale, limit, cuts=(), kind=jnp.bfloat16):
    result = scale * jax.random.normal(stream_key, extent, jnp.float32)
    if cuts:
        result = result * steps_of(stream_key, extent, cuts, -0.22, 0.18)
    return jnp.clip(result, -limit, limit).astype(kind)


def setup_inputs(seed: int = 0) -> dict:
    keys = jax.random.split(jax.random.key(seed), 4)
    return {
        "layer_input": centred(keys[0], (TOKENS, D), 1.0, 6.0, ((0, 16), (1, 16))),
        "pairs": draw_pairs(jax.random.fold_in(keys[3], 71), 0),
        "counts": ragged_sizes(keys[2], READERS, READERS * LB * 5 // 8, LB, 2).astype(jnp.int32),
    }


def band_row(padded, layer_input, row_block):
    start = (row_block * BS).astype(jnp.int32)
    left = lax.dynamic_slice_in_dim(layer_input, start, BS, 1)
    window = lax.dynamic_slice_in_dim(padded, start, (2 * BAND - 1) * BS, 1)
    return lax.dot_general(left, window, (((0,), (0,)), ((), ())), preferred_element_type=jnp.float32)


def reference(layer_input, pairs, counts):
    margin = (BAND - 1) * BS
    padded = jnp.pad(layer_input, ((0, 0), (margin, margin)))
    band_blocks = lax.map(partial(band_row, padded, layer_input), jnp.arange(NB, dtype=jnp.int32))

    def pick_block(row_block, col_block):
        offset = ((col_block - row_block + BAND - 1) * BS).astype(jnp.int32)
        zero_start = jnp.zeros((), jnp.int32)
        return lax.dynamic_slice(band_blocks, (row_block.astype(jnp.int32), zero_start, offset), (1, BS, BS))[0]

    picked = jax.vmap(jax.vmap(pick_block))(pairs[0], pairs[1])
    live_slots = jnp.arange(LB, dtype=jnp.int32)[None, :] < counts[:, None]
    weighted = picked * (2.0 / TOKENS)
    return jnp.where(live_slots[:, :, None, None], weighted, jnp.zeros_like(weighted))
```

```python
import functools
import jax
import jax.numpy as jnp
from jax import lax
from jax.experimental import pallas as pl
from jax.experimental.pallas import tpu as pltpu
from jax.sharding import PartitionSpec as P

BS = 256
BAND = 4
NX, NY, NZ = 4, 4, 8
CHIPS = NX * NY
CHUNKS = 4
MESH = pl.DeviceIdType.MESH

TABLE = {
    (0, 0): (0, 0), (0, 1): (1, 0), (1, 1): (2, 0),
    (2, 2): (3, 0), (2, 3): (4, 0), (3, 3): (5, 0),
    (1, 4): (6, 0), (3, 6): (7, 0),
    (0, 2): (8, 0), (0, 3): (9, 0), (1, 2): (10, 0), (1, 3): (11, 0),
    (0, -2): (12, 0), (0, -1): (13, 0), (1, -2): (14, 0), (1, -1): (15, 0),
    (2, 4): (16, 1), (3, 4): (17, 1), (2, 5): (18, 1), (3, 5): (19, 1),
    (0, -3): (20, 1), (2, -1): (21, 1),
    (1, 0): (1, 1), (3, 2): (4, 1),
    (2, 0): (8, 1), (3, 0): (9, 1), (2, 1): (10, 1), (3, 1): (11, 1),
}
WIDTH = 2 * BAND - 1


def device(x, y, z, k):
    return (((x % 2) * NY + y) * 2 + k, z, x // 2)


def gram(a, b):
    return lax.dot_general(a, b, (((0,), (0,)), ((), ())), preferred_element_type=jnp.float32)


def kernel(
    weight, x_ref, pairs_ref, counts_ref, out_ref,
    own, cross, below, ahead, p_own, p_mid, p_low, k_own, k_mid, k_low,
    r_own, r_mid, r_low, table, stage, arrived, pairs_far, pairs_all, lookup,
    local_sem, x_send, x_recv, zf_send, zf_recv, ze_send, ze_recv, pr_send, pr_recv,
    core_send, core_recv, rs_send, rs_recv, hop_send, hop_recv, out_send, out_recv,
):
    token = lax.axis_index("token")
    z = lax.axis_index("brow")
    c = lax.axis_index("bcol")
    k = token % 2
    y = (token // 2) % NY
    x = 2 * c + token // (2 * NY)
    me = y * NX + x
    half = x_ref.shape[0] // 2
    step = half // CHUNKS
    up, down = (z + 1) % NZ, (z + NZ - 1) % NZ

    load = pltpu.make_async_copy(x_ref, own, local_sem.at[0])
    load.start()
    load_pairs = pltpu.make_async_copy(pairs_ref, pairs_all.at[c], local_sem.at[1])
    load_pairs.start()

    barrier = pltpu.get_barrier_semaphore()

    def plane_peer(o):
        return (x + o % NX) % NX, (y + (o // NX) % NY) % NY, (k + o // CHIPS) % 2

    def greet(o, carry):
        px, py, pk = plane_peer(o)
        pl.semaphore_signal(barrier, inc=1, device_id=device(px, py, z, pk), device_id_type=MESH)
        return carry

    lax.fori_loop(1, 2 * CHIPS, greet, 0)
    pl.semaphore_signal(barrier, inc=1, device_id=device(x, y, up, k), device_id_type=MESH)
    pl.semaphore_signal(barrier, inc=1, device_id=device(x, y, down, k), device_id_type=MESH)
    for (row, col), (at, flip) in TABLE.items():
        lookup[row * WIDTH + col - row + BAND - 1] = at * 2 + flip
    pl.semaphore_wait(barrier, 2 * CHIPS + 1)

    def x_copy(direction, j):
        to = device((x + 1) % NX, y, z, k) if direction == 0 else device((x + NX - 1) % NX, y, z, k)
        first = (c if direction == 0 else 1 - c) * half + j * step
        return pltpu.make_async_remote_copy(
            src_ref=x_ref.at[pl.ds(first, step), :],
            dst_ref=cross.at[c, pl.ds(j * step, step), :],
            send_sem=x_send.at[direction, j],
            recv_sem=x_recv.at[c, j],
            device_id=to, device_id_type=MESH,
        )

    def x_arrival(side, j):
        return pltpu.make_async_remote_copy(
            src_ref=x_ref.at[pl.ds(0, step), :],
            dst_ref=cross.at[side, pl.ds(j * step, step), :],
            send_sem=x_send.at[0, j],
            recv_sem=x_recv.at[side, j],
            device_id=device((x + 1) % NX, y, z, k), device_id_type=MESH,
        )

    def forward(j):
        return pltpu.make_async_remote_copy(
            src_ref=cross.at[1, pl.ds(j * step, step), :],
            dst_ref=below.at[pl.ds(j * step, step), :],
            send_sem=zf_send.at[j], recv_sem=zf_recv.at[j],
            device_id=device(x, y, up, k), device_id_type=MESH,
        )

    for j in range(CHUNKS):
        x_copy(0, j).start()
        x_copy(1, j).start()
    edge = pltpu.make_async_remote_copy(
        src_ref=x_ref.at[:, pl.ds(0, BS)], dst_ref=ahead,
        send_sem=ze_send, recv_sem=ze_recv,
        device_id=device(x, y, down, k), device_id_type=MESH,
    )
    edge.start()
    share_pairs = pltpu.make_async_remote_copy(
        src_ref=pairs_ref, dst_ref=pairs_far, send_sem=pr_send, recv_sem=pr_recv,
        device_id=device((x + 2) % NX, y, z, k), device_id_type=MESH,
    )
    share_pairs.start()

    def put(ref, q, value):
        ref[:, :, :, q * 8 : q * 8 + 8, :] = value.reshape(2, NY, NX, 8, BS)

    def to_sibling(g, part, got):
        return pltpu.make_async_remote_copy(
            src_ref=part.at[1 - k], dst_ref=got,
            send_sem=core_send.at[g], recv_sem=core_recv.at[g],
            device_id=device(x, y, z, 1 - k), device_id_type=MESH,
        )

    def scatter_copy(g, got, land, o):
        px, py = (x + o % NX) % NX, (y + o // NX) % NY
        return pltpu.make_async_remote_copy(
            src_ref=got.at[py, px], dst_ref=land.at[me],
            send_sem=rs_send.at[g, o], recv_sem=rs_recv.at[g, me],
            device_id=device(px, py, z, k), device_id_type=MESH,
        )

    def scatter_arrival(g, got, land, o):
        px, py = (x + o % NX) % NX, (y + o // NX) % NY
        source = py * NX + px
        return pltpu.make_async_remote_copy(
            src_ref=got.at[py, px], dst_ref=land.at[source],
            send_sem=rs_send.at[g, o], recv_sem=rs_recv.at[g, source],
            device_id=device(px, py, z, k), device_id_type=MESH,
        )

    def scatter(g, part, got, land):
        copy = to_sibling(g, part, got)
        copy.wait()
        for row in range(NY):
            got[row] = got[row] + part[k, row]

        def send(o, carry):
            scatter_copy(g, got, land, o).start()
            return carry

        lax.fori_loop(1, CHIPS, send, 0)
        land[me] = got[y, x]

    def collect(g, got, land):
        def take(o, carry):
            scatter_arrival(g, got, land, o).wait_recv()
            return carry

        lax.fori_loop(1, CHIPS, take, 0)

    load.wait()
    put(p_own, 0, gram(own[:, :BS], own[:, :BS]))
    put(p_own, 1, gram(own[:, :BS], own[:, BS:]))
    put(p_own, 2, gram(own[:, BS:], own[:, BS:]))
    to_sibling(0, p_own, k_own).start()

    for j in range(CHUNKS):
        x_arrival(1, j).wait_recv()
        forward(j).start()
    scatter(0, p_own, k_own, r_own)
    for j in range(CHUNKS):
        x_arrival(0, j).wait_recv()

    for i in range(2):
        for j in range(2):
            put(p_mid, 1 + 2 * i + j, gram(cross[0, :, i * BS : (i + 1) * BS], cross[1, :, j * BS : (j + 1) * BS]))
    edge.wait_recv()
    put(p_mid, 0, gram(own[:, BS:], ahead[...]))
    to_sibling(1, p_mid, k_mid).start()
    scatter(1, p_mid, k_mid, r_mid)

    for j in range(CHUNKS):
        forward(j).wait_recv()
    for i in range(2):
        for j in range(2):
            put(p_low, 2 * i + j, gram(cross[0, :, i * BS : (i + 1) * BS], below[:, j * BS : (j + 1) * BS]))
    to_sibling(2, p_low, k_low).start()
    scatter(2, p_low, k_low, r_low)

    share_pairs.wait_recv()
    load_pairs.wait()
    far = pltpu.make_async_copy(pairs_far, pairs_all.at[1 - c], local_sem.at[2])
    far.start()

    collect(0, k_own, r_own)
    for side in range(2):
        total = None
        for row in range(NY):
            for col in range(2):
                term = r_own[row * NX + 2 * side + col]
                total = term if total is None else total + term
        table[3 * side : 3 * side + 3] = total.reshape(3, 8, BS)
    collect(1, k_mid, r_mid)
    for side in range(2):
        total = None
        for row in range(NY):
            for col in range(2):
                term = r_mid[row * NX + 2 * side + col, 0:8, :]
                total = term if total is None else total + term
        table[6 + side] = total
    hop_up = pltpu.make_async_remote_copy(
        src_ref=table.at[pl.ds(6, 2)], dst_ref=table.at[pl.ds(20, 2)],
        send_sem=hop_send.at[0], recv_sem=hop_recv.at[0],
        device_id=device(x, y, up, k), device_id_type=MESH,
    )
    hop_up.start()
    total = r_mid[0, 8:40, :]
    for source in range(1, CHIPS):
        total = total + r_mid[source, 8:40, :]
    table[8:12] = total.reshape(4, 8, BS)
    collect(2, k_low, r_low)
    total = r_low[0]
    for source in range(1, CHIPS):
        total = total + r_low[source]
    table[12:16] = total.reshape(4, 8, BS)
    hop_down = pltpu.make_async_remote_copy(
        src_ref=table.at[pl.ds(12, 4)], dst_ref=table.at[pl.ds(16, 4)],
        send_sem=hop_send.at[1], recv_sem=hop_recv.at[1],
        device_id=device(x, y, down, k), device_id_type=MESH,
    )
    hop_down.start()
    far.wait()
    hop_up.wait()
    hop_down.wait()

    def code(reader, slot):
        row = pairs_all[reader, 0, 0, slot]
        col = pairs_all[reader, 1, 0, slot]
        at = (row - z * BAND) * WIDTH + col - row + BAND - 1
        return lookup[jnp.clip(at, 0, BAND * WIDTH - 1)]

    def fill(o, px, py, pk):
        slot = 2 * (((px % 2) * NY + py) * 2 + pk)
        reader = px // 2
        stage[o, 0] = table[code(reader, slot) // 2]
        stage[o, 1] = table[code(reader, slot + 1) // 2]

    rank = k * CHIPS + me

    def deliver(o):
        px, py, pk = plane_peer(o)
        return pltpu.make_async_remote_copy(
            src_ref=stage.at[o], dst_ref=arrived.at[rank],
            send_sem=out_send.at[o], recv_sem=out_recv.at[rank],
            device_id=device(px, py, z, pk), device_id_type=MESH,
        )

    def send_out(o, carry):
        px, py, pk = plane_peer(o)
        fill(o, px, py, pk)
        deliver(o).start()
        return carry

    lax.fori_loop(1, 2 * CHIPS, send_out, 0)
    fill(0, x, y, k)
    arrived[rank] = stage[0]

    def take_out(o, carry):
        px, py, pk = plane_peer(o)
        source = pk * CHIPS + py * NX + px
        pltpu.make_async_remote_copy(
            src_ref=stage.at[o], dst_ref=arrived.at[source],
            send_sem=out_send.at[o], recv_sem=out_recv.at[source],
            device_id=device(px, py, z, pk), device_id_type=MESH,
        ).wait_recv()
        return carry

    lax.fori_loop(1, 2 * CHIPS, take_out, 0)
    for s in range(2):
        slot = 2 * token + s
        block = arrived[:, s].reshape(BS, BS)
        flip = code(c, slot) % 2 == 1
        block = jnp.where(flip, block.T, block)
        out_ref[0, s] = jnp.where(slot < counts_ref[0], block * weight, 0.0)

    for j in range(CHUNKS):
        x_copy(0, j).wait_send()
        x_copy(1, j).wait_send()
        forward(j).wait_send()
    edge.wait_send()
    share_pairs.wait_send()
    for g, (got, land) in enumerate(((k_own, r_own), (k_mid, r_mid), (k_low, r_low))):
        def left(o, carry):
            scatter_copy(g, got, land, o).wait_send()
            return carry

        lax.fori_loop(1, CHIPS, left, 0)

    def left_out(o, carry):
        deliver(o).wait_send()
        return carry

    lax.fori_loop(1, 2 * CHIPS, left_out, 0)


def shards(layer_input, pairs, counts):
    rows, columns = layer_input.shape
    weight = 2.0 / (rows * lax.axis_size("token"))
    dma, vmem = pltpu.SemaphoreType.DMA, pltpu.VMEM
    f32, bf16 = jnp.float32, jnp.bfloat16
    slots = pairs.shape[2] // lax.axis_size("token")
    scratch = [
        vmem((rows, columns), bf16),
        vmem((2, rows // 2, columns), bf16),
        vmem((rows // 2, columns), bf16),
        vmem((rows, BS), bf16),
    ]
    heights = (24, 40, 32)
    scratch += [vmem((2, NY, NX, h, BS), f32) for h in heights]
    scratch += [vmem((NY, NX, h, BS), f32) for h in heights]
    scratch += [vmem((CHIPS, h, BS), f32) for h in heights]
    scratch += [
        vmem((22, 8, BS), f32),
        vmem((2 * CHIPS, slots, 8, BS), f32),
        vmem((2 * CHIPS, slots, 8, BS), f32),
        vmem(pairs.shape, jnp.int32),
        pltpu.SMEM((2,) + pairs.shape, jnp.int32),
        pltpu.SMEM((BAND * WIDTH,), jnp.int32),
        dma((3,)),
        dma((2, CHUNKS)), dma((2, CHUNKS)),
        dma((CHUNKS,)), dma((CHUNKS,)),
        dma, dma, dma, dma,
        dma((3,)), dma((3,)),
        dma((3, CHIPS)), dma((3, CHIPS)),
        dma((2,)), dma((2,)),
        dma((2 * CHIPS,)), dma((2 * CHIPS,)),
    ]
    return pl.pallas_call(
        functools.partial(kernel, weight),
        out_shape=jax.ShapeDtypeStruct((1, slots, BS, BS), f32),
        in_specs=[
            pl.BlockSpec(memory_space=pl.ANY),
            pl.BlockSpec(memory_space=pl.ANY),
            pl.BlockSpec(memory_space=pltpu.SMEM),
        ],
        out_specs=pl.BlockSpec(memory_space=pltpu.VMEM),
        scratch_shapes=scratch,
        compiler_params=pltpu.CompilerParams(
            collective_id=0, has_side_effects=True, vmem_limit_bytes=48 * 2**20
        ),
    )(layer_input, pairs, counts)


def solution(mesh):
    return jax.shard_map(
        shards,
        mesh=mesh,
        in_specs=(
            P("token", ("brow", "bcol")),
            P(None, ("brow", "bcol"), None),
            P(("brow", "bcol")),
        ),
        out_specs=P(("brow", "bcol"), "token", None, None),
        check_vma=False,
    )
```

```python
import functools
import jax
import jax.numpy as jnp
from jax import lax
from jax.experimental import pallas as pl
from jax.experimental.pallas import tpu as pltpu
from jax.sharding import PartitionSpec as P

BS = 256
BAND = 4
NX, NY, NZ = 4, 4, 8
CHIPS = NX * NY
CHUNKS = 8
WINDOW = 3
MESH = pl.DeviceIdType.MESH

TABLE = {
    (0, 0): (0, 0), (0, 1): (1, 0), (1, 1): (2, 0),
    (2, 2): (3, 0), (2, 3): (4, 0), (3, 3): (5, 0),
    (1, 4): (6, 0), (3, 6): (7, 0),
    (0, 2): (8, 0), (0, 3): (9, 0), (1, 2): (10, 0), (1, 3): (11, 0),
    (0, -2): (12, 0), (0, -1): (13, 0), (1, -2): (14, 0), (1, -1): (15, 0),
    (2, 4): (16, 1), (3, 4): (17, 1), (2, 5): (18, 1), (3, 5): (19, 1),
    (0, -3): (20, 1), (2, -1): (21, 1),
    (1, 0): (1, 1), (3, 2): (4, 1),
    (2, 0): (8, 1), (3, 0): (9, 1), (2, 1): (10, 1), (3, 1): (11, 1),
}
WIDTH = 2 * BAND - 1


def device(x, y, z, k):
    return (((x % 2) * NY + y) * 2 + k, z, x // 2)


def gram(a, b):
    return lax.dot_general(a, b, (((0,), (0,)), ((), ())), preferred_element_type=jnp.float32)


def kernel(
    weight, x_ref, pairs_ref, counts_ref, out_ref,
    own, cross, below, ahead, p_own, p_mid, p_low, k_own, k_mid, k_low,
    r_own, r_mid, r_low, table, stage, arrived, pairs_far, pairs_all, lookup,
    local_sem, x_send, x_recv, zf_send, zf_recv, ze_send, ze_recv, pr_send, pr_recv,
    core_send, core_recv, y_own, s_own, y_send, y_recv, row_send, row_recv, rs_send, rs_recv, hop_send, hop_recv, out_send, out_recv,
):
    token = lax.axis_index("token")
    z = lax.axis_index("brow")
    c = lax.axis_index("bcol")
    k = token % 2
    y = (token // 2) % NY
    x = 2 * c + token // (2 * NY)
    me = y * NX + x
    half = x_ref.shape[0] // 2
    step = half // CHUNKS
    up, down = (z + 1) % NZ, (z + NZ - 1) % NZ

    load = pltpu.make_async_copy(x_ref, own, local_sem.at[0])
    load.start()
    load_pairs = pltpu.make_async_copy(pairs_ref, pairs_all.at[c], local_sem.at[1])
    load_pairs.start()

    barrier = pltpu.get_barrier_semaphore()

    def plane_peer(o):
        return (x + o % NX) % NX, (y + (o // NX) % NY) % NY, (k + o // CHIPS) % 2

    near = [device((x + o) % NX, y, z, k) for o in (2, 1, 3)]
    near += [device(x, (y + o) % NY, z, k) for o in (2, 1, 3)]
    near += [device(x, y, up, k), device(x, y, down, k), device(x, y, z, 1 - k)]
    for peer in near:
        pl.semaphore_signal(barrier, inc=1, device_id=peer, device_id_type=MESH)
    for (row, col), (at, flip) in TABLE.items():
        lookup[row * WIDTH + col - row + BAND - 1] = at * 2 + flip
    pl.semaphore_wait(barrier, len(near))

    def x_copy(direction, j):
        to = device((x + 1) % NX, y, z, k) if direction == 0 else device((x + NX - 1) % NX, y, z, k)
        first = (c if direction == 0 else 1 - c) * half + j * step
        return pltpu.make_async_remote_copy(
            src_ref=x_ref.at[pl.ds(first, step), :],
            dst_ref=cross.at[c, pl.ds(j * step, step), :],
            send_sem=x_send.at[direction, j],
            recv_sem=x_recv.at[c, j],
            device_id=to, device_id_type=MESH,
        )

    def x_arrival(side, j):
        return pltpu.make_async_remote_copy(
            src_ref=x_ref.at[pl.ds(0, step), :],
            dst_ref=cross.at[side, pl.ds(j * step, step), :],
            send_sem=x_send.at[0, j],
            recv_sem=x_recv.at[side, j],
            device_id=device((x + 1) % NX, y, z, k), device_id_type=MESH,
        )

    def forward(j):
        return pltpu.make_async_remote_copy(
            src_ref=cross.at[1, pl.ds(j * step, step), :],
            dst_ref=below.at[pl.ds(j * step, step), :],
            send_sem=zf_send.at[j], recv_sem=zf_recv.at[j],
            device_id=device(x, y, up, k), device_id_type=MESH,
        )

    for j in range(WINDOW):
        x_copy(0, j).start()
        x_copy(1, j).start()
    edge = pltpu.make_async_remote_copy(
        src_ref=x_ref.at[:, pl.ds(0, BS)], dst_ref=ahead,
        send_sem=ze_send, recv_sem=ze_recv,
        device_id=device(x, y, down, k), device_id_type=MESH,
    )
    edge.start()
    share_pairs = pltpu.make_async_remote_copy(
        src_ref=pairs_ref, dst_ref=pairs_far, send_sem=pr_send, recv_sem=pr_recv,
        device_id=device((x + 2) % NX, y, z, k), device_id_type=MESH,
    )
    share_pairs.start()

    def put(ref, q, value):
        ref[:, :, :, q * 8 : q * 8 + 8, :] = value.reshape(2, NY, NX, 8, BS)

    def to_sibling(g, part, got):
        return pltpu.make_async_remote_copy(
            src_ref=part.at[1 - k], dst_ref=got,
            send_sem=core_send.at[g], recv_sem=core_recv.at[g],
            device_id=device(x, y, z, 1 - k), device_id_type=MESH,
        )

    def scatter_copy(g, got, land, o):
        px, py = (x + o % NX) % NX, (y + o // NX) % NY
        return pltpu.make_async_remote_copy(
            src_ref=got.at[py, px], dst_ref=land.at[me],
            send_sem=rs_send.at[g, o], recv_sem=rs_recv.at[g, me],
            device_id=device(px, py, z, k), device_id_type=MESH,
        )

    def scatter_arrival(g, got, land, o):
        px, py = (x + o % NX) % NX, (y + o // NX) % NY
        source = py * NX + px
        return pltpu.make_async_remote_copy(
            src_ref=got.at[py, px], dst_ref=land.at[source],
            send_sem=rs_send.at[g, o], recv_sem=rs_recv.at[g, source],
            device_id=device(px, py, z, k), device_id_type=MESH,
        )

    def scatter(g, part, got, land):
        copy = to_sibling(g, part, got)
        copy.wait()
        for row in range(NY):
            got[row] = got[row] + part[k, row]

        def send(o, carry):
            scatter_copy(g, got, land, o).start()
            return carry

        lax.fori_loop(1, CHIPS, send, 0)
        land[me] = got[y, x]

    def collect(g, got, land):
        def take(o, carry):
            scatter_arrival(g, got, land, o).wait_recv()
            return carry

        lax.fori_loop(1, CHIPS, take, 0)

    def y_copy(o, source):
        return pltpu.make_async_remote_copy(
            src_ref=k_own.at[(y + o) % NY], dst_ref=y_own.at[source],
            send_sem=y_send.at[o], recv_sem=y_recv.at[source],
            device_id=device(x, (y + o) % NY, z, k), device_id_type=MESH,
        )

    def row_copy(o, source):
        return pltpu.make_async_remote_copy(
            src_ref=s_own.at[(x + o) % NX], dst_ref=r_own.at[source],
            send_sem=row_send.at[o], recv_sem=row_recv.at[source],
            device_id=device((x + o) % NX, y, z, k), device_id_type=MESH,
        )

    def own_along_y():
        to_sibling(0, p_own, k_own).wait()
        for row in range(NY):
            k_own[row] = k_own[row] + p_own[k, row]
        for o in range(1, NY):
            y_copy(o, y).start()
        y_own[y] = k_own[y]

    def own_along_x():
        for o in range(1, NY):
            y_copy(o, (y + o) % NY).wait_recv()
        s_own[...] = (y_own[0] + y_own[1]) + (y_own[2] + y_own[3])
        for o in range(1, NX):
            row_copy(o, x).start()
        r_own[x] = s_own[x]

    load.wait()
    put(p_own, 0, gram(own[:, :BS], own[:, :BS]))
    put(p_own, 1, gram(own[:, :BS], own[:, BS:]))
    put(p_own, 2, gram(own[:, BS:], own[:, BS:]))
    to_sibling(0, p_own, k_own).start()

    for j in range(CHUNKS):
        x_arrival(1, j).wait_recv()
        forward(j).start()
        x_copy(0, j).wait_send()
        x_copy(1, j).wait_send()
        if j + WINDOW < CHUNKS:
            x_copy(0, j + WINDOW).start()
            x_copy(1, j + WINDOW).start()
        if j == 0:
            own_along_y()
        if j == CHUNKS - 3:
            own_along_x()
    for j in range(CHUNKS):
        x_arrival(0, j).wait_recv()
    share_pairs.wait_recv()
    load_pairs.wait()
    far = pltpu.make_async_copy(pairs_far, pairs_all.at[1 - c], local_sem.at[2])
    far.start()

    for i in range(2):
        for j in range(2):
            put(p_mid, 1 + 2 * i + j, gram(cross[0, :, i * BS : (i + 1) * BS], cross[1, :, j * BS : (j + 1) * BS]))
    edge.wait_recv()
    put(p_mid, 0, gram(own[:, BS:], ahead[...]))
    to_sibling(1, p_mid, k_mid).start()
    scatter(1, p_mid, k_mid, r_mid)

    for j in range(CHUNKS):
        forward(j).wait_recv()
    for i in range(2):
        for j in range(2):
            put(p_low, 2 * i + j, gram(cross[0, :, i * BS : (i + 1) * BS], below[:, j * BS : (j + 1) * BS]))
    to_sibling(2, p_low, k_low).start()
    scatter(2, p_low, k_low, r_low)

    for o in range(1, NX):
        row_copy(o, (x + o) % NX).wait_recv()
    for side in range(2):
        table[3 * side : 3 * side + 3] = (r_own[2 * side] + r_own[2 * side + 1]).reshape(3, 8, BS)
    collect(1, k_mid, r_mid)
    for side in range(2):
        total = None
        for row in range(NY):
            for col in range(2):
                term = r_mid[row * NX + 2 * side + col, 0:8, :]
                total = term if total is None else total + term
        table[6 + side] = total
    hop_up = pltpu.make_async_remote_copy(
        src_ref=table.at[pl.ds(6, 2)], dst_ref=table.at[pl.ds(20, 2)],
        send_sem=hop_send.at[0], recv_sem=hop_recv.at[0],
        device_id=device(x, y, up, k), device_id_type=MESH,
    )
    hop_up.start()
    total = r_mid[0, 8:40, :]
    for source in range(1, CHIPS):
        total = total + r_mid[source, 8:40, :]
    table[8:12] = total.reshape(4, 8, BS)
    collect(2, k_low, r_low)
    total = r_low[0]
    for source in range(1, CHIPS):
        total = total + r_low[source]
    table[12:16] = total.reshape(4, 8, BS)
    hop_down = pltpu.make_async_remote_copy(
        src_ref=table.at[pl.ds(12, 4)], dst_ref=table.at[pl.ds(16, 4)],
        send_sem=hop_send.at[1], recv_sem=hop_recv.at[1],
        device_id=device(x, y, down, k), device_id_type=MESH,
    )
    hop_down.start()
    far.wait()
    hop_up.wait()
    hop_down.wait()

    def code(reader, slot):
        row = pairs_all[reader, 0, 0, slot]
        col = pairs_all[reader, 1, 0, slot]
        at = (row - z * BAND) * WIDTH + col - row + BAND - 1
        return lookup[jnp.clip(at, 0, BAND * WIDTH - 1)]

    def fill(o, px, py, pk):
        slot = 2 * (((px % 2) * NY + py) * 2 + pk)
        reader = px // 2
        stage[o, 0] = table[code(reader, slot) // 2]
        stage[o, 1] = table[code(reader, slot + 1) // 2]

    rank = k * CHIPS + me

    def deliver(o):
        px, py, pk = plane_peer(o)
        return pltpu.make_async_remote_copy(
            src_ref=stage.at[o], dst_ref=arrived.at[rank],
            send_sem=out_send.at[o], recv_sem=out_recv.at[rank],
            device_id=device(px, py, z, pk), device_id_type=MESH,
        )

    def send_out(o, carry):
        px, py, pk = plane_peer(o)
        fill(o, px, py, pk)
        deliver(o).start()
        return carry

    lax.fori_loop(1, 2 * CHIPS, send_out, 0)
    fill(0, x, y, k)
    arrived[rank] = stage[0]

    def take_out(o, carry):
        px, py, pk = plane_peer(o)
        source = pk * CHIPS + py * NX + px
        pltpu.make_async_remote_copy(
            src_ref=stage.at[o], dst_ref=arrived.at[source],
            send_sem=out_send.at[o], recv_sem=out_recv.at[source],
            device_id=device(px, py, z, pk), device_id_type=MESH,
        ).wait_recv()
        return carry

    lax.fori_loop(1, 2 * CHIPS, take_out, 0)
    for s in range(2):
        slot = 2 * token + s
        block = arrived[:, s].reshape(BS, BS)
        flip = code(c, slot) % 2 == 1
        block = jnp.where(flip, block.T, block)
        out_ref[0, s] = jnp.where(slot < counts_ref[0], block * weight, 0.0)

    for j in range(CHUNKS):
        forward(j).wait_send()
    for o in range(1, NY):
        y_copy(o, y).wait_send()
    for o in range(1, NX):
        row_copy(o, x).wait_send()
    edge.wait_send()
    share_pairs.wait_send()
    for g, got, land in ((1, k_mid, r_mid), (2, k_low, r_low)):
        def left(o, carry):
            scatter_copy(g, got, land, o).wait_send()
            return carry

        lax.fori_loop(1, CHIPS, left, 0)

    def left_out(o, carry):
        deliver(o).wait_send()
        return carry

    lax.fori_loop(1, 2 * CHIPS, left_out, 0)


def shards(layer_input, pairs, counts):
    rows, columns = layer_input.shape
    weight = 2.0 / (rows * lax.axis_size("token"))
    dma, vmem = pltpu.SemaphoreType.DMA, pltpu.VMEM
    f32, bf16 = jnp.float32, jnp.bfloat16
    slots = pairs.shape[2] // lax.axis_size("token")
    scratch = [
        vmem((rows, columns), bf16),
        vmem((2, rows // 2, columns), bf16),
        vmem((rows // 2, columns), bf16),
        vmem((rows, BS), bf16),
    ]
    heights = (24, 40, 32)
    scratch += [vmem((2, NY, NX, h, BS), f32) for h in heights]
    scratch += [vmem((NY, NX, h, BS), f32) for h in heights]
    scratch += [vmem((n, h, BS), f32) for n, h in zip((NX, CHIPS, CHIPS), heights)]
    scratch += [
        vmem((22, 8, BS), f32),
        vmem((2 * CHIPS, slots, 8, BS), f32),
        vmem((2 * CHIPS, slots, 8, BS), f32),
        vmem(pairs.shape, jnp.int32),
        pltpu.SMEM((2,) + pairs.shape, jnp.int32),
        pltpu.SMEM((BAND * WIDTH,), jnp.int32),
        dma((3,)),
        dma((2, CHUNKS)), dma((2, CHUNKS)),
        dma((CHUNKS,)), dma((CHUNKS,)),
        dma, dma, dma, dma,
        dma((3,)), dma((3,)),
        vmem((NY, NX, heights[0], BS), f32), vmem((NX, heights[0], BS), f32),
        dma((NY,)), dma((NY,)), dma((NX,)), dma((NX,)),
        dma((3, CHIPS)), dma((3, CHIPS)),
        dma((2,)), dma((2,)),
        dma((2 * CHIPS,)), dma((2 * CHIPS,)),
    ]
    return pl.pallas_call(
        functools.partial(kernel, weight),
        out_shape=jax.ShapeDtypeStruct((1, slots, BS, BS), f32),
        in_specs=[
            pl.BlockSpec(memory_space=pltpu.HBM),
            pl.BlockSpec(memory_space=pltpu.HBM),
            pl.BlockSpec(memory_space=pltpu.SMEM),
        ],
        out_specs=pl.BlockSpec(memory_space=pltpu.VMEM),
        scratch_shapes=scratch,
        compiler_params=pltpu.CompilerParams(
            collective_id=0, has_side_effects=True, vmem_limit_bytes=62 * 2**20
        ),
    )(layer_input, pairs, counts)


def solution(mesh):
    return jax.shard_map(
        shards,
        mesh=mesh,
        in_specs=(
            P("token", ("brow", "bcol")),
            P(None, ("brow", "bcol"), None),
            P(("brow", "bcol")),
        ),
        out_specs=P(("brow", "bcol"), "token", None, None),
        check_vma=False,
    )
```

```python
import functools
import jax
import jax.numpy as jnp
from jax import lax
from jax.experimental import pallas as pl
from jax.experimental.pallas import tpu as pltpu
from jax.sharding import PartitionSpec as P

BS = 256
BAND = 4
NX, NY, NZ = 4, 4, 8
CHIPS = NX * NY
CHUNKS = 8
PARTS = 4
MESH = pl.DeviceIdType.MESH

TABLE = {
    (0, 0): (0, 0), (0, 1): (1, 0), (1, 1): (2, 0),
    (2, 2): (3, 0), (2, 3): (4, 0), (3, 3): (5, 0),
    (1, 4): (6, 0), (3, 6): (7, 0),
    (0, 2): (8, 0), (0, 3): (9, 0), (1, 2): (10, 0), (1, 3): (11, 0),
    (0, -2): (12, 0), (0, -1): (13, 0), (1, -2): (14, 0), (1, -1): (15, 0),
    (2, 4): (16, 1), (3, 4): (17, 1), (2, 5): (18, 1), (3, 5): (19, 1),
    (0, -3): (20, 1), (2, -1): (21, 1),
    (1, 0): (1, 1), (3, 2): (4, 1),
    (2, 0): (8, 1), (3, 0): (9, 1), (2, 1): (10, 1), (3, 1): (11, 1),
}
WIDTH = 2 * BAND - 1


def device(x, y, z, k):
    return (((x % 2) * NY + y) * 2 + k, z, x // 2)


def gram(a, b):
    return lax.dot_general(a, b, (((0,), (0,)), ((), ())), preferred_element_type=jnp.float32)


def kernel(
    weight, x_ref, pairs_ref, counts_ref, out_ref,
    own, cross, below, ahead, far_rows, far_cols, far_below, far_own, far_ahead,
    p_own, k_own, p_mid, p_low, r_own, r_mid, r_low, table, stage, arrived, pairs_far, pairs_all, lookup,
    local_sem, x_send, x_recv, zf_send, zf_recv, ze_send, ze_recv, pr_send, pr_recv,
    core_send, core_recv, swap_send, swap_recv, y_own, s_own, y_send, y_recv, row_send, row_recv, rs_send, rs_recv, hop_send, hop_recv, out_send, out_recv,
):
    token = lax.axis_index("token")
    z = lax.axis_index("brow")
    c = lax.axis_index("bcol")
    k = token % 2
    y = (token // 2) % NY
    x = 2 * c + token // (2 * NY)
    me = y * NX + x
    half = x_ref.shape[0] // 2
    step = half // CHUNKS
    up, down = (z + 1) % NZ, (z + NZ - 1) % NZ

    load = pltpu.make_async_copy(x_ref, own, local_sem.at[0])
    load.start()
    load_pairs = pltpu.make_async_copy(pairs_ref, pairs_all.at[c], local_sem.at[1])
    load_pairs.start()

    barrier = pltpu.get_barrier_semaphore()

    def plane_peer(o):
        return (x + o % NX) % NX, (y + (o // NX) % NY) % NY, (k + o // CHIPS) % 2

    near = [device((x + o) % NX, y, z, k) for o in (2, 1, 3)]
    near += [device(x, (y + o) % NY, z, k) for o in (2, 1, 3)]
    near += [device(x, y, up, k), device(x, y, down, k), device(x, y, z, 1 - k)]
    for peer in near:
        pl.semaphore_signal(barrier, inc=1, device_id=peer, device_id_type=MESH)
    for (row, col), (at, flip) in TABLE.items():
        lookup[row * WIDTH + col - row + BAND - 1] = at * 2 + flip
    pl.semaphore_wait(barrier, len(near))

    def x_copy(direction, j):
        to = device((x + 1) % NX, y, z, k) if direction == 0 else device((x + NX - 1) % NX, y, z, k)
        first = (c if direction == 0 else 1 - c) * half + j * step
        return pltpu.make_async_remote_copy(
            src_ref=x_ref.at[pl.ds(first, step), :],
            dst_ref=cross.at[c, pl.ds(j * step, step), :],
            send_sem=x_send.at[direction, j],
            recv_sem=x_recv.at[c, j],
            device_id=to, device_id_type=MESH,
        )

    def x_arrival(side, j):
        return pltpu.make_async_remote_copy(
            src_ref=x_ref.at[pl.ds(0, step), :],
            dst_ref=cross.at[side, pl.ds(j * step, step), :],
            send_sem=x_send.at[0, j],
            recv_sem=x_recv.at[side, j],
            device_id=device((x + 1) % NX, y, z, k), device_id_type=MESH,
        )

    def forward(j):
        return pltpu.make_async_remote_copy(
            src_ref=cross.at[1, pl.ds(j * step, step), :],
            dst_ref=below.at[pl.ds(j * step, step), :],
            send_sem=zf_send.at[j], recv_sem=zf_recv.at[j],
            device_id=device(x, y, up, k), device_id_type=MESH,
        )

    for j in range(CHUNKS):
        x_copy(0, j).start()
        x_copy(1, j).start()
    edge = pltpu.make_async_remote_copy(
        src_ref=x_ref.at[:, pl.ds(0, BS)], dst_ref=ahead,
        send_sem=ze_send, recv_sem=ze_recv,
        device_id=device(x, y, down, k), device_id_type=MESH,
    )
    edge.start()
    share_pairs = pltpu.make_async_remote_copy(
        src_ref=pairs_ref, dst_ref=pairs_far, send_sem=pr_send, recv_sem=pr_recv,
        device_id=device((x + 2) % NX, y, z, k), device_id_type=MESH,
    )
    share_pairs.start()

    def swap(n, source, target):
        return pltpu.make_async_remote_copy(
            src_ref=source, dst_ref=target,
            send_sem=swap_send.at[n], recv_sem=swap_recv.at[n],
            device_id=device(x, y, z, 1 - k), device_id_type=MESH,
        )

    def strip(ref, block, core, *lead):
        first = pl.multiple_of(block * BS + core * (BS // 2), BS // 2)
        return ref.at[lead + (slice(None), pl.ds(first, BS // 2))]

    part = half // PARTS

    def swap_rows(g, i):
        rows = pl.ds(g * part, part)
        first = pl.multiple_of(i * BS + (1 - k) * (BS // 2), BS // 2)
        return swap(
            2 * g + i, cross.at[0, rows, pl.ds(first, BS // 2)],
            far_rows.at[rows, i * (BS // 2) : (i + 1) * (BS // 2)],
        )

    def swap_cols(g):
        rows = pl.ds(g * part, part)
        return swap(2 * PARTS + g, cross.at[1, rows, :], far_cols.at[rows, :])

    def swap_below(g):
        rows = pl.ds(g * part, part)
        return swap(3 * PARTS + g, below.at[rows, :], far_below.at[rows, :])

    swap_own = swap(4 * PARTS, strip(own, 1, 1 - k), far_own)
    swap_ahead = swap(4 * PARTS + 1, ahead, far_ahead)

    def put(ref, q, value):
        ref[..., q * 8 : q * 8 + 8, :] = value.reshape(ref.shape[:-2] + (8, BS))

    def to_sibling():
        return pltpu.make_async_remote_copy(
            src_ref=p_own.at[1 - k], dst_ref=k_own,
            send_sem=core_send, recv_sem=core_recv,
            device_id=device(x, y, z, 1 - k), device_id_type=MESH,
        )

    def scatter_copy(g, got, land, o):
        px, py = (x + o % NX) % NX, (y + o // NX) % NY
        return pltpu.make_async_remote_copy(
            src_ref=got.at[py, px], dst_ref=land.at[me],
            send_sem=rs_send.at[g, o], recv_sem=rs_recv.at[g, me],
            device_id=device(px, py, z, k), device_id_type=MESH,
        )

    def scatter_arrival(g, got, land, o):
        px, py = (x + o % NX) % NX, (y + o // NX) % NY
        source = py * NX + px
        return pltpu.make_async_remote_copy(
            src_ref=got.at[py, px], dst_ref=land.at[source],
            send_sem=rs_send.at[g, o], recv_sem=rs_recv.at[g, source],
            device_id=device(px, py, z, k), device_id_type=MESH,
        )

    def scatter(g, got, land):
        def send(o, carry):
            scatter_copy(g, got, land, o).start()
            return carry

        lax.fori_loop(1, CHIPS, send, 0)
        land[me] = got[y, x]

    def collect(g, got, land):
        def take(o, carry):
            scatter_arrival(g, got, land, o).wait_recv()
            return carry

        lax.fori_loop(1, CHIPS, take, 0)

    def y_copy(o, source):
        return pltpu.make_async_remote_copy(
            src_ref=k_own.at[(y + o) % NY], dst_ref=y_own.at[source],
            send_sem=y_send.at[o], recv_sem=y_recv.at[source],
            device_id=device(x, (y + o) % NY, z, k), device_id_type=MESH,
        )

    def row_copy(o, source):
        return pltpu.make_async_remote_copy(
            src_ref=s_own.at[(x + o) % NX], dst_ref=r_own.at[source],
            send_sem=row_send.at[o], recv_sem=row_recv.at[source],
            device_id=device((x + o) % NX, y, z, k), device_id_type=MESH,
        )

    def own_along_y():
        to_sibling().wait()
        for row in range(NY):
            k_own[row] = k_own[row] + p_own[k, row]
        for o in range(1, NY):
            y_copy(o, y).start()
        y_own[y] = k_own[y]

    def own_along_x():
        for o in range(1, NY):
            y_copy(o, (y + o) % NY).wait_recv()
        s_own[...] = (y_own[0] + y_own[1]) + (y_own[2] + y_own[3])
        for o in range(1, NX):
            row_copy(o, x).start()
        r_own[x] = s_own[x]

    load.wait()
    swap_own.start()
    put(p_own, 0, gram(own[:, :BS], own[:, :BS]))
    put(p_own, 1, gram(own[:, :BS], own[:, BS:]))
    put(p_own, 2, gram(own[:, BS:], own[:, BS:]))
    to_sibling().start()

    for j in range(CHUNKS):
        x_arrival(1, j).wait_recv()
        forward(j).start()
        x_arrival(0, j).wait_recv()
        if (j + 1) % (CHUNKS // PARTS) == 0:
            g = j // (CHUNKS // PARTS)
            swap_rows(g, 0).start()
            swap_rows(g, 1).start()
            swap_cols(g).start()
        if j == 0:
            own_along_y()
        if j == CHUNKS - 3:
            own_along_x()
    share_pairs.wait_recv()
    load_pairs.wait()
    far = pltpu.make_async_copy(pairs_far, pairs_all.at[1 - c], local_sem.at[2])
    far.start()

    for g in range(PARTS):
        swap_rows(g, 0).wait_recv()
        swap_rows(g, 1).wait_recv()
        swap_cols(g).wait_recv()

    near_rows = jnp.concatenate([strip(cross, 0, k, 0)[...], strip(cross, 1, k, 0)[...]], axis=1)

    def put_pairs(ref, near, far):
        for j in range(2):
            cols = slice(j * BS, (j + 1) * BS)
            both = gram(near_rows, near[:, cols]) + gram(far_rows[...], far[:, cols])
            put(ref, j, both[: BS // 2])
            put(ref, 2 + j, both[BS // 2 :])

    put_pairs(p_mid, cross.at[1], far_cols)
    scatter(0, p_mid, r_mid)

    edge.wait_recv()
    swap_ahead.start()
    for g in range(PARTS):
        for j in range(g * CHUNKS // PARTS, (g + 1) * CHUNKS // PARTS):
            forward(j).wait_recv()
        swap_below(g).start()
    swap_own.wait_recv()
    swap_ahead.wait_recv()
    put(p_low, 4, gram(strip(own, 1, k)[...], ahead[...]) + gram(far_own[...], far_ahead[...]))
    for g in range(PARTS):
        swap_below(g).wait_recv()
    put_pairs(p_low, below, far_below)
    scatter(1, p_low, r_low)

    for o in range(1, NX):
        row_copy(o, (x + o) % NX).wait_recv()
    for side in range(2):
        table[3 * side : 3 * side + 3] = (r_own[2 * side] + r_own[2 * side + 1]).reshape(3, 8, BS)
    collect(0, p_mid, r_mid)

    def add(land, at):
        def one(q, carry):
            rows = pl.ds(pl.multiple_of(q * 8, 8), 8)
            terms = [land[source, rows, :] for source in range(CHIPS)]
            while len(terms) > 1:
                terms = [a + b for a, b in zip(terms[::2], terms[1::2])]
            table[at + q] = terms[0]
            return carry

        lax.fori_loop(0, 4, one, 0)

    add(r_mid, 8)
    collect(1, p_low, r_low)
    add(r_low, 12)
    hop_down = pltpu.make_async_remote_copy(
        src_ref=table.at[pl.ds(12, 4)], dst_ref=table.at[pl.ds(16, 4)],
        send_sem=hop_send.at[1], recv_sem=hop_recv.at[1],
        device_id=device(x, y, down, k), device_id_type=MESH,
    )
    hop_down.start()
    for side in range(2):
        total = None
        for row in range(NY):
            for col in range(2):
                term = r_low[row * NX + 2 * side + col, 32:40, :]
                total = term if total is None else total + term
        table[6 + side] = total
    hop_up = pltpu.make_async_remote_copy(
        src_ref=table.at[pl.ds(6, 2)], dst_ref=table.at[pl.ds(20, 2)],
        send_sem=hop_send.at[0], recv_sem=hop_recv.at[0],
        device_id=device(x, y, up, k), device_id_type=MESH,
    )
    hop_up.start()
    far.wait()
    hop_up.wait()
    hop_down.wait()

    def code(reader, slot):
        row = pairs_all[reader, 0, 0, slot]
        col = pairs_all[reader, 1, 0, slot]
        at = (row - z * BAND) * WIDTH + col - row + BAND - 1
        return lookup[jnp.clip(at, 0, BAND * WIDTH - 1)]

    def fill(o, px, py, pk):
        slot = 2 * (((px % 2) * NY + py) * 2 + pk)
        reader = px // 2
        stage[o, 0] = table[code(reader, slot) // 2]
        stage[o, 1] = table[code(reader, slot + 1) // 2]

    rank = k * CHIPS + me

    def deliver(o):
        px, py, pk = plane_peer(o)
        return pltpu.make_async_remote_copy(
            src_ref=stage.at[o], dst_ref=arrived.at[rank],
            send_sem=out_send.at[o], recv_sem=out_recv.at[rank],
            device_id=device(px, py, z, pk), device_id_type=MESH,
        )

    def send_out(o, carry):
        px, py, pk = plane_peer(o)
        fill(o, px, py, pk)
        deliver(o).start()
        return carry

    lax.fori_loop(1, 2 * CHIPS, send_out, 0)
    fill(0, x, y, k)
    arrived[rank] = stage[0]

    def take_out(o, carry):
        px, py, pk = plane_peer(o)
        source = pk * CHIPS + py * NX + px
        pltpu.make_async_remote_copy(
            src_ref=stage.at[o], dst_ref=arrived.at[source],
            send_sem=out_send.at[o], recv_sem=out_recv.at[source],
            device_id=device(px, py, z, pk), device_id_type=MESH,
        ).wait_recv()
        return carry

    lax.fori_loop(1, 2 * CHIPS, take_out, 0)
    for s in range(2):
        slot = 2 * token + s
        block = arrived[:, s].reshape(BS, BS)
        flip = code(c, slot) % 2 == 1
        block = jnp.where(flip, block.T, block)
        out_ref[0, s] = jnp.where(slot < counts_ref[0], block * weight, 0.0)

    for j in range(CHUNKS):
        x_copy(0, j).wait_send()
        x_copy(1, j).wait_send()
        forward(j).wait_send()
    for g in range(PARTS):
        swap_rows(g, 0).wait_send()
        swap_rows(g, 1).wait_send()
        swap_cols(g).wait_send()
        swap_below(g).wait_send()
    swap_own.wait_send()
    swap_ahead.wait_send()
    for o in range(1, NY):
        y_copy(o, y).wait_send()
    for o in range(1, NX):
        row_copy(o, x).wait_send()
    edge.wait_send()
    share_pairs.wait_send()
    for g, got, land in ((0, p_mid, r_mid), (1, p_low, r_low)):
        def left(o, carry):
            scatter_copy(g, got, land, o).wait_send()
            return carry

        lax.fori_loop(1, CHIPS, left, 0)

    def left_out(o, carry):
        deliver(o).wait_send()
        return carry

    lax.fori_loop(1, 2 * CHIPS, left_out, 0)


def shards(layer_input, pairs, counts):
    rows, columns = layer_input.shape
    weight = 2.0 / (rows * lax.axis_size("token"))
    dma, vmem = pltpu.SemaphoreType.DMA, pltpu.VMEM
    f32, bf16 = jnp.float32, jnp.bfloat16
    slots = pairs.shape[2] // lax.axis_size("token")
    scratch = [
        vmem((rows, columns), bf16),
        vmem((2, rows // 2, columns), bf16),
        vmem((rows // 2, columns), bf16),
        vmem((rows, BS), bf16),
    ]
    scratch += [
        vmem((rows // 2, BS), bf16),
        vmem((rows // 2, columns), bf16),
        vmem((rows // 2, columns), bf16),
        vmem((rows, BS // 2), bf16),
        vmem((rows, BS), bf16),
        vmem((2, NY, NX, 24, BS), f32), vmem((NY, NX, 24, BS), f32),
        vmem((NY, NX, 32, BS), f32), vmem((NY, NX, 40, BS), f32),
        vmem((NX, 24, BS), f32), vmem((CHIPS, 32, BS), f32), vmem((CHIPS, 40, BS), f32),
    ]
    scratch += [
        vmem((22, 8, BS), f32),
        vmem((2 * CHIPS, slots, 8, BS), f32),
        vmem((2 * CHIPS, slots, 8, BS), f32),
        vmem(pairs.shape, jnp.int32),
        pltpu.SMEM((2,) + pairs.shape, jnp.int32),
        pltpu.SMEM((BAND * WIDTH,), jnp.int32),
        dma((3,)),
        dma((2, CHUNKS)), dma((2, CHUNKS)),
        dma((CHUNKS,)), dma((CHUNKS,)),
        dma, dma, dma, dma,
        dma, dma, dma((4 * PARTS + 2,)), dma((4 * PARTS + 2,)),
        vmem((NY, NX, 24, BS), f32), vmem((NX, 24, BS), f32),
        dma((NY,)), dma((NY,)), dma((NX,)), dma((NX,)),
        dma((2, CHIPS)), dma((2, CHIPS)),
        dma((2,)), dma((2,)),
        dma((2 * CHIPS,)), dma((2 * CHIPS,)),
    ]
    return pl.pallas_call(
        functools.partial(kernel, weight),
        out_shape=jax.ShapeDtypeStruct((1, slots, BS, BS), f32),
        in_specs=[
            pl.BlockSpec(memory_space=pltpu.HBM),
            pl.BlockSpec(memory_space=pltpu.HBM),
            pl.BlockSpec(memory_space=pltpu.SMEM),
        ],
        out_specs=pl.BlockSpec(memory_space=pltpu.VMEM),
        scratch_shapes=scratch,
        compiler_params=pltpu.CompilerParams(
            collective_id=0, has_side_effects=True, vmem_limit_bytes=252 * 2**18
        ),
    )(layer_input, pairs, counts)


def solution(mesh):
    return jax.shard_map(
        shards,
        mesh=mesh,
        in_specs=(
            P("token", ("brow", "bcol")),
            P(None, ("brow", "bcol"), None),
            P(("brow", "bcol")),
        ),
        out_specs=P(("brow", "bcol"), "token", None, None),
        check_vma=False,
    )
```

```python
import functools
import jax
import jax.numpy as jnp
from jax import lax
from jax.experimental import pallas as pl
from jax.experimental.pallas import tpu as pltpu
from jax.sharding import PartitionSpec as P

BS = 256
BAND = 4
NX, NY, NZ = 4, 4, 8
CHIPS = NX * NY
CHUNKS = 8
PARTS = 4
MESH = pl.DeviceIdType.MESH

TABLE = {
    (0, 0): (0, 0), (0, 1): (1, 0), (1, 1): (2, 0),
    (2, 2): (3, 0), (2, 3): (4, 0), (3, 3): (5, 0),
    (1, 4): (6, 0), (3, 6): (7, 0),
    (0, 2): (8, 0), (0, 3): (9, 0), (1, 2): (10, 0), (1, 3): (11, 0),
    (0, -2): (12, 0), (0, -1): (13, 0), (1, -2): (14, 0), (1, -1): (15, 0),
    (2, 4): (16, 1), (3, 4): (17, 1), (2, 5): (18, 1), (3, 5): (19, 1),
    (0, -3): (20, 1), (2, -1): (21, 1),
    (1, 0): (1, 1), (3, 2): (4, 1),
    (2, 0): (8, 1), (3, 0): (9, 1), (2, 1): (10, 1), (3, 1): (11, 1),
}
WIDTH = 2 * BAND - 1


def device(x, y, z, k):
    return (((x % 2) * NY + y) * 2 + k, z, x // 2)


def gram(a, b):
    return lax.dot_general(a, b, (((0,), (0,)), ((), ())), preferred_element_type=jnp.float32)


def exponents(peak):
    return jnp.ceil(8.0 * jnp.log2(jnp.maximum(peak, 1e-30) * (1.0 / 32000.0)))


def spread(rows):
    return jnp.concatenate([jnp.broadcast_to(row, (8, BS)) for row in rows], axis=0)


def to_i16(value):
    return jnp.floor(value + 0.5).astype(jnp.int32).astype(jnp.int16)


def to_f32(value):
    return value.astype(jnp.int32).astype(jnp.float32)


def kernel(
    weight, x_ref, pairs_ref, counts_ref, out_ref,
    own, cross, below, ahead, far_rows, far_cols, far_below, far_own, far_ahead,
    p_own, k_own, p_mid, p_low, q_mid, q_low, scales, r_own, r_mid, r_low, grow, table, stage, arrived, pairs_far, pairs_all, lookup,
    local_sem, x_send, x_recv, zf_send, zf_recv, ze_send, ze_recv, pr_send, pr_recv,
    core_send, core_recv, swap_send, swap_recv, y_own, s_own, y_send, y_recv, row_send, row_recv, rs_send, rs_recv, hop_send, hop_recv, out_send, out_recv,
):
    token = lax.axis_index("token")
    z = lax.axis_index("brow")
    c = lax.axis_index("bcol")
    k = token % 2
    y = (token // 2) % NY
    x = 2 * c + token // (2 * NY)
    me = y * NX + x
    half = x_ref.shape[0] // 2
    step = half // CHUNKS
    up, down = (z + 1) % NZ, (z + NZ - 1) % NZ

    load = pltpu.make_async_copy(x_ref, own, local_sem.at[0])
    load.start()
    load_pairs = pltpu.make_async_copy(pairs_ref, pairs_all.at[c], local_sem.at[1])
    load_pairs.start()

    barrier = pltpu.get_barrier_semaphore()

    def plane_peer(o):
        return (x + o % NX) % NX, (y + (o // NX) % NY) % NY, (k + o // CHIPS) % 2

    near = [device((x + o) % NX, y, z, k) for o in (2, 1, 3)]
    near += [device(x, (y + o) % NY, z, k) for o in (2, 1, 3)]
    near += [device(x, y, up, k), device(x, y, down, k), device(x, y, z, 1 - k)]
    for peer in near:
        pl.semaphore_signal(barrier, inc=1, device_id=peer, device_id_type=MESH)
    for (row, col), (at, flip) in TABLE.items():
        lookup[row * WIDTH + col - row + BAND - 1] = at * 2 + flip
    pl.semaphore_wait(barrier, len(near))

    def x_copy(direction, j):
        to = device((x + 1) % NX, y, z, k) if direction == 0 else device((x + NX - 1) % NX, y, z, k)
        first = (c if direction == 0 else 1 - c) * half + j * step
        return pltpu.make_async_remote_copy(
            src_ref=x_ref.at[pl.ds(first, step), :],
            dst_ref=cross.at[c, pl.ds(j * step, step), :],
            send_sem=x_send.at[direction, j],
            recv_sem=x_recv.at[c, j],
            device_id=to, device_id_type=MESH,
        )

    def x_arrival(side, j):
        return pltpu.make_async_remote_copy(
            src_ref=x_ref.at[pl.ds(0, step), :],
            dst_ref=cross.at[side, pl.ds(j * step, step), :],
            send_sem=x_send.at[0, j],
            recv_sem=x_recv.at[side, j],
            device_id=device((x + 1) % NX, y, z, k), device_id_type=MESH,
        )

    def forward(j):
        return pltpu.make_async_remote_copy(
            src_ref=cross.at[1, pl.ds(j * step, step), :],
            dst_ref=below.at[pl.ds(j * step, step), :],
            send_sem=zf_send.at[j], recv_sem=zf_recv.at[j],
            device_id=device(x, y, up, k), device_id_type=MESH,
        )

    for j in range(CHUNKS):
        x_copy(0, j).start()
        x_copy(1, j).start()
    edge = pltpu.make_async_remote_copy(
        src_ref=x_ref.at[:, pl.ds(0, BS)], dst_ref=ahead,
        send_sem=ze_send, recv_sem=ze_recv,
        device_id=device(x, y, down, k), device_id_type=MESH,
    )
    edge.start()
    share_pairs = pltpu.make_async_remote_copy(
        src_ref=pairs_ref, dst_ref=pairs_far, send_sem=pr_send, recv_sem=pr_recv,
        device_id=device((x + 2) % NX, y, z, k), device_id_type=MESH,
    )
    share_pairs.start()

    def swap(n, source, target):
        return pltpu.make_async_remote_copy(
            src_ref=source, dst_ref=target,
            send_sem=swap_send.at[n], recv_sem=swap_recv.at[n],
            device_id=device(x, y, z, 1 - k), device_id_type=MESH,
        )

    def strip(ref, block, core, *lead):
        first = pl.multiple_of(block * BS + core * (BS // 2), BS // 2)
        return ref.at[lead + (slice(None), pl.ds(first, BS // 2))]

    part = half // PARTS

    def swap_rows(g, i):
        rows = pl.ds(g * part, part)
        first = pl.multiple_of(i * BS + (1 - k) * (BS // 2), BS // 2)
        return swap(
            2 * g + i, cross.at[0, rows, pl.ds(first, BS // 2)],
            far_rows.at[rows, i * (BS // 2) : (i + 1) * (BS // 2)],
        )

    def swap_cols(g):
        rows = pl.ds(g * part, part)
        return swap(2 * PARTS + g, cross.at[1, rows, :], far_cols.at[rows, :])

    def swap_below(g):
        rows = pl.ds(g * part, part)
        return swap(3 * PARTS + g, below.at[rows, :], far_below.at[rows, :])

    swap_own = swap(4 * PARTS, strip(own, 1, 1 - k), far_own)
    swap_ahead = swap(4 * PARTS + 1, ahead, far_ahead)

    def put(ref, q, value):
        ref[..., q * 8 : q * 8 + 8, :] = value.reshape(ref.shape[:-2] + (8, BS))

    def to_sibling():
        return pltpu.make_async_remote_copy(
            src_ref=p_own.at[1 - k], dst_ref=k_own,
            send_sem=core_send, recv_sem=core_recv,
            device_id=device(x, y, z, 1 - k), device_id_type=MESH,
        )

    def scatter_copy(g, got, land, o):
        px, py = (x + o % NX) % NX, (y + o // NX) % NY
        return pltpu.make_async_remote_copy(
            src_ref=got.at[py, px], dst_ref=land.at[me],
            send_sem=rs_send.at[g, o], recv_sem=rs_recv.at[g, me],
            device_id=device(px, py, z, k), device_id_type=MESH,
        )

    def scatter_arrival(g, got, land, o):
        px, py = (x + o % NX) % NX, (y + o // NX) % NY
        source = py * NX + px
        return pltpu.make_async_remote_copy(
            src_ref=got.at[py, px], dst_ref=land.at[source],
            send_sem=rs_send.at[g, o], recv_sem=rs_recv.at[g, source],
            device_id=device(px, py, z, k), device_id_type=MESH,
        )

    def scatter(g, got, land):
        def send(o, carry):
            scatter_copy(g, got, land, o).start()
            return carry

        lax.fori_loop(1, CHIPS, send, 0)
        land[me] = got[y, x]

    def collect(g, got, land):
        def take(o, carry):
            scatter_arrival(g, got, land, o).wait_recv()
            return carry

        lax.fori_loop(1, CHIPS, take, 0)

    def y_copy(o, source):
        return pltpu.make_async_remote_copy(
            src_ref=k_own.at[(y + o) % NY], dst_ref=y_own.at[source],
            send_sem=y_send.at[o], recv_sem=y_recv.at[source],
            device_id=device(x, (y + o) % NY, z, k), device_id_type=MESH,
        )

    def row_copy(o, source):
        return pltpu.make_async_remote_copy(
            src_ref=s_own.at[(x + o) % NX], dst_ref=r_own.at[source],
            send_sem=row_send.at[o], recv_sem=row_recv.at[source],
            device_id=device((x + o) % NX, y, z, k), device_id_type=MESH,
        )

    def own_along_y():
        to_sibling().wait()
        for row in range(NY):
            k_own[row] = k_own[row] + p_own[k, row]
        for o in range(1, NY):
            y_copy(o, y).start()
        y_own[y] = k_own[y]

    def own_along_x():
        for o in range(1, NY):
            y_copy(o, (y + o) % NY).wait_recv()
        s_own[...] = (y_own[0] + y_own[1]) + (y_own[2] + y_own[3])
        for o in range(1, NX):
            row_copy(o, x).start()
        r_own[x] = s_own[x]

    load.wait()
    swap_own.start()
    put(p_own, 0, gram(own[:, :BS], own[:, :BS]))
    put(p_own, 1, gram(own[:, :BS], own[:, BS:]))
    put(p_own, 2, gram(own[:, BS:], own[:, BS:]))
    to_sibling().start()

    for j in range(CHUNKS):
        x_arrival(1, j).wait_recv()
        forward(j).start()
        x_arrival(0, j).wait_recv()
        if (j + 1) % (CHUNKS // PARTS) == 0:
            g = j // (CHUNKS // PARTS)
            swap_rows(g, 0).start()
            swap_rows(g, 1).start()
            swap_cols(g).start()
        if j == 0:
            own_along_y()
        if j == CHUNKS - 3:
            own_along_x()
    share_pairs.wait_recv()
    load_pairs.wait()
    far = pltpu.make_async_copy(pairs_far, pairs_all.at[1 - c], local_sem.at[2])
    far.start()

    for g in range(PARTS):
        swap_rows(g, 0).wait_recv()
        swap_rows(g, 1).wait_recv()
        swap_cols(g).wait_recv()

    near_rows = jnp.concatenate([strip(cross, 0, k, 0)[...], strip(cross, 1, k, 0)[...]], axis=1)

    def put_pairs(ref, near, far):
        for j in range(2):
            cols = slice(j * BS, (j + 1) * BS)
            both = gram(near_rows, near[:, cols]) + gram(far_rows[...], far[:, cols])
            put(ref, j, both[: BS // 2])
            put(ref, 2 + j, both[BS // 2 :])

    put_pairs(p_mid, cross.at[1], far_cols)

    def peak(ref, q):
        top = None
        for row in range(NY):
            for col in range(NX):
                size = jnp.abs(ref[row, col, q * 8 : q * 8 + 8, :])
                top = size if top is None else jnp.maximum(top, size)
        return jnp.max(top, axis=0, keepdims=True)

    rows = [exponents(peak(p_mid, q)) for q in range(4)]
    for q in range(4):
        scales[q : q + 1, :] = rows[q]
    shrink = spread([jnp.exp2(row * -0.125) for row in rows])
    for row in range(NY):
        for col in range(NX):
            q_mid[row, col] = to_i16(p_mid[row, col] * shrink)
    scatter(0, q_mid, r_mid)

    edge.wait_recv()
    swap_ahead.start()
    for g in range(PARTS):
        for j in range(g * CHUNKS // PARTS, (g + 1) * CHUNKS // PARTS):
            forward(j).wait_recv()
        swap_below(g).start()
    swap_own.wait_recv()
    swap_ahead.wait_recv()
    put(p_low, 4, gram(strip(own, 1, k)[...], ahead[...]) + gram(far_own[...], far_ahead[...]))
    for g in range(PARTS):
        swap_below(g).wait_recv()
    put_pairs(p_low, below, far_below)
    rows = [exponents(jnp.maximum(peak(p_low, q), peak(p_low, 2 + q))) for q in range(2)]
    rows.append(exponents(peak(p_low, 4)))
    for q in range(3):
        scales[4 + q : 5 + q, :] = rows[q]
    scales[7:8, :] = jnp.zeros((1, BS), jnp.float32)
    shrink = spread([jnp.exp2(rows[q] * -0.125) for q in (0, 1, 0, 1, 2)])
    for row in range(NY):
        for col in range(NX):
            q_low[row, col] = to_i16(jnp.concatenate([p_low[row, col] * shrink, scales[...]], axis=0))
    scatter(1, q_low, r_low)

    for o in range(1, NX):
        row_copy(o, (x + o) % NX).wait_recv()
    for side in range(2):
        table[3 * side : 3 * side + 3] = (r_own[2 * side] + r_own[2 * side + 1]).reshape(3, 8, BS)
    collect(1, q_low, r_low)
    edges, sums = [None, None], None
    for source in range(CHIPS):
        tail = to_f32(r_low[source, 32:48, :])
        grow[source] = jnp.exp2(tail[8:16, :] * 0.125)
        term = to_f32(r_low[source, 0:32, :]) * spread([grow[source, q : q + 1, :] for q in (4, 5, 4, 5)])
        sums = term if sums is None else sums + term
        edge_term = tail[0:8, :] * grow[source, 6:7, :]
        side = source % NX // 2
        edges[side] = edge_term if edges[side] is None else edges[side] + edge_term
    table[12:16] = sums.reshape(4, 8, BS)
    hop_down = pltpu.make_async_remote_copy(
        src_ref=table.at[pl.ds(12, 4)], dst_ref=table.at[pl.ds(16, 4)],
        send_sem=hop_send.at[1], recv_sem=hop_recv.at[1],
        device_id=device(x, y, down, k), device_id_type=MESH,
    )
    hop_down.start()
    table[6] = edges[0]
    table[7] = edges[1]
    hop_up = pltpu.make_async_remote_copy(
        src_ref=table.at[pl.ds(6, 2)], dst_ref=table.at[pl.ds(20, 2)],
        send_sem=hop_send.at[0], recv_sem=hop_recv.at[0],
        device_id=device(x, y, up, k), device_id_type=MESH,
    )
    hop_up.start()
    collect(0, q_mid, r_mid)
    sums = None
    for source in range(CHIPS):
        term = to_f32(r_mid[source]) * spread([grow[source, q : q + 1, :] for q in range(4)])
        sums = term if sums is None else sums + term
    table[8:12] = sums.reshape(4, 8, BS)
    far.wait()
    hop_up.wait()
    hop_down.wait()

    def code(reader, slot):
        row = pairs_all[reader, 0, 0, slot]
        col = pairs_all[reader, 1, 0, slot]
        at = (row - z * BAND) * WIDTH + col - row + BAND - 1
        return lookup[jnp.clip(at, 0, BAND * WIDTH - 1)]

    def fill(o, px, py, pk):
        slot = 2 * (((px % 2) * NY + py) * 2 + pk)
        reader = px // 2
        stage[o, 0] = table[code(reader, slot) // 2]
        stage[o, 1] = table[code(reader, slot + 1) // 2]

    rank = k * CHIPS + me

    def deliver(o):
        px, py, pk = plane_peer(o)
        return pltpu.make_async_remote_copy(
            src_ref=stage.at[o], dst_ref=arrived.at[rank],
            send_sem=out_send.at[o], recv_sem=out_recv.at[rank],
            device_id=device(px, py, z, pk), device_id_type=MESH,
        )

    def send_out(o, carry):
        px, py, pk = plane_peer(o)
        fill(o, px, py, pk)
        deliver(o).start()
        return carry

    lax.fori_loop(1, 2 * CHIPS, send_out, 0)
    fill(0, x, y, k)
    arrived[rank] = stage[0]

    def take_out(o, carry):
        px, py, pk = plane_peer(o)
        source = pk * CHIPS + py * NX + px
        pltpu.make_async_remote_copy(
            src_ref=stage.at[o], dst_ref=arrived.at[source],
            send_sem=out_send.at[o], recv_sem=out_recv.at[source],
            device_id=device(px, py, z, pk), device_id_type=MESH,
        ).wait_recv()
        return carry

    lax.fori_loop(1, 2 * CHIPS, take_out, 0)
    for s in range(2):
        slot = 2 * token + s
        block = arrived[:, s].reshape(BS, BS)
        flip = code(c, slot) % 2 == 1
        block = jnp.where(flip, block.T, block)
        out_ref[0, s] = jnp.where(slot < counts_ref[0], block * weight, 0.0)

    for j in range(CHUNKS):
        x_copy(0, j).wait_send()
        x_copy(1, j).wait_send()
        forward(j).wait_send()
    for g in range(PARTS):
        swap_rows(g, 0).wait_send()
        swap_rows(g, 1).wait_send()
        swap_cols(g).wait_send()
        swap_below(g).wait_send()
    swap_own.wait_send()
    swap_ahead.wait_send()
    for o in range(1, NY):
        y_copy(o, y).wait_send()
    for o in range(1, NX):
        row_copy(o, x).wait_send()
    edge.wait_send()
    share_pairs.wait_send()
    for g, got, land in ((0, q_mid, r_mid), (1, q_low, r_low)):
        def left(o, carry):
            scatter_copy(g, got, land, o).wait_send()
            return carry

        lax.fori_loop(1, CHIPS, left, 0)

    def left_out(o, carry):
        deliver(o).wait_send()
        return carry

    lax.fori_loop(1, 2 * CHIPS, left_out, 0)


def shards(layer_input, pairs, counts):
    rows, columns = layer_input.shape
    weight = 2.0 / (rows * lax.axis_size("token"))
    dma, vmem = pltpu.SemaphoreType.DMA, pltpu.VMEM
    f32, bf16, i16 = jnp.float32, jnp.bfloat16, jnp.int16
    slots = pairs.shape[2] // lax.axis_size("token")
    scratch = [
        vmem((rows, columns), bf16),
        vmem((2, rows // 2, columns), bf16),
        vmem((rows // 2, columns), bf16),
        vmem((rows, BS), bf16),
    ]
    scratch += [
        vmem((rows // 2, BS), bf16),
        vmem((rows // 2, columns), bf16),
        vmem((rows // 2, columns), bf16),
        vmem((rows, BS // 2), bf16),
        vmem((rows, BS), bf16),
        vmem((2, NY, NX, 24, BS), f32), vmem((NY, NX, 24, BS), f32),
        vmem((NY, NX, 32, BS), f32), vmem((NY, NX, 40, BS), f32),
        vmem((NY, NX, 32, BS), i16), vmem((NY, NX, 48, BS), i16), vmem((8, BS), f32),
        vmem((NX, 24, BS), f32), vmem((CHIPS, 32, BS), i16), vmem((CHIPS, 48, BS), i16),
        vmem((CHIPS, 8, BS), f32),
    ]
    scratch += [
        vmem((22, 8, BS), f32),
        vmem((2 * CHIPS, slots, 8, BS), f32),
        vmem((2 * CHIPS, slots, 8, BS), f32),
        vmem(pairs.shape, jnp.int32),
        pltpu.SMEM((2,) + pairs.shape, jnp.int32),
        pltpu.SMEM((BAND * WIDTH,), jnp.int32),
        dma((3,)),
        dma((2, CHUNKS)), dma((2, CHUNKS)),
        dma((CHUNKS,)), dma((CHUNKS,)),
        dma, dma, dma, dma,
        dma, dma, dma((4 * PARTS + 2,)), dma((4 * PARTS + 2,)),
        vmem((NY, NX, 24, BS), f32), vmem((NX, 24, BS), f32),
        dma((NY,)), dma((NY,)), dma((NX,)), dma((NX,)),
        dma((2, CHIPS)), dma((2, CHIPS)),
        dma((2,)), dma((2,)),
        dma((2 * CHIPS,)), dma((2 * CHIPS,)),
    ]
    return pl.pallas_call(
        functools.partial(kernel, weight),
        out_shape=jax.ShapeDtypeStruct((1, slots, BS, BS), f32),
        in_specs=[
            pl.BlockSpec(memory_space=pltpu.HBM),
            pl.BlockSpec(memory_space=pltpu.HBM),
            pl.BlockSpec(memory_space=pltpu.SMEM),
        ],
        out_specs=pl.BlockSpec(memory_space=pltpu.VMEM),
        scratch_shapes=scratch,
        compiler_params=pltpu.CompilerParams(
            collective_id=0, has_side_effects=True, vmem_limit_bytes=252 * 2**18
        ),
    )(layer_input, pairs, counts)


def solution(mesh):
    return jax.shard_map(
        shards,
        mesh=mesh,
        in_specs=(
            P("token", ("brow", "bcol")),
            P(None, ("brow", "bcol"), None),
            P(("brow", "bcol")),
        ),
        out_specs=P(("brow", "bcol"), "token", None, None),
        check_vma=False,
    )
```

```python
import functools
import jax
import jax.numpy as jnp
from jax import lax
from jax.experimental import pallas as pl
from jax.experimental.pallas import tpu as pltpu
from jax.sharding import PartitionSpec as P

BS = 256
BAND = 4
NX, NY, NZ = 4, 4, 8
CHIPS = NX * NY
CHUNKS = 8
PARTS = 4
MESH = pl.DeviceIdType.MESH

TABLE = {
    (0, 0): (0, 0), (0, 1): (1, 0), (1, 1): (2, 0),
    (2, 2): (3, 0), (2, 3): (4, 0), (3, 3): (5, 0),
    (1, 4): (6, 0), (3, 6): (7, 0),
    (0, 2): (8, 0), (0, 3): (9, 0), (1, 2): (10, 0), (1, 3): (11, 0),
    (0, -2): (12, 0), (0, -1): (13, 0), (1, -2): (14, 0), (1, -1): (15, 0),
    (2, 4): (16, 1), (3, 4): (17, 1), (2, 5): (18, 1), (3, 5): (19, 1),
    (0, -3): (20, 1), (2, -1): (21, 1),
    (1, 0): (1, 1), (3, 2): (4, 1),
    (2, 0): (8, 1), (3, 0): (9, 1), (2, 1): (10, 1), (3, 1): (11, 1),
}
WIDTH = 2 * BAND - 1


def device(x, y, z, k):
    return (((x % 2) * NY + y) * 2 + k, z, x // 2)


def gram(a, b):
    return lax.dot_general(a, b, (((0,), (0,)), ((), ())), preferred_element_type=jnp.float32)


def far_first(n):
    return (2 + 3 * n + 3 * (n * (n - 1) // 2)) % 4


def exponents(peak):
    return jnp.ceil(8.0 * jnp.log2(jnp.maximum(peak, 1e-30) * (1.0 / 32000.0)))


def spread(rows):
    return jnp.concatenate([jnp.broadcast_to(row, (8, BS)) for row in rows], axis=0)


def to_i16(value):
    return jnp.floor(value + 0.5).astype(jnp.int32).astype(jnp.int16)


def to_f32(value):
    return value.astype(jnp.int32).astype(jnp.float32)


def kernel(
    weight, x_ref, pairs_ref, counts_ref, out_ref,
    own, cross, below, ahead, far_rows, far_cols, far_below, far_own, far_ahead,
    p_own, k_own, p_mid, p_low, q_mid, q_low, scales, r_own, r_mid, r_low, grow, table, packed, blocks, stage, arrived, pairs_far, pairs_all, lookup,
    local_sem, x_send, x_recv, zf_send, zf_recv, ze_send, ze_recv, pr_send, pr_recv,
    core_send, core_recv, swap_send, swap_recv, y_own, s_own, y_send, y_recv, row_send, row_recv, rs_send, rs_recv, hop_send, hop_recv, out_send, out_recv,
):
    token = lax.axis_index("token")
    z = lax.axis_index("brow")
    c = lax.axis_index("bcol")
    k = token % 2
    y = (token // 2) % NY
    x = 2 * c + token // (2 * NY)
    me = y * NX + x
    half = x_ref.shape[0] // 2
    step = half // CHUNKS
    up, down = (z + 1) % NZ, (z + NZ - 1) % NZ

    load = pltpu.make_async_copy(x_ref, own, local_sem.at[0])
    load.start()
    load_pairs = pltpu.make_async_copy(pairs_ref, pairs_all.at[c], local_sem.at[1])
    load_pairs.start()

    barrier = pltpu.get_barrier_semaphore()

    def chip_peer(o):
        return (x + far_first(o % NX)) % NX, (y + far_first(o // NX)) % NY

    def plane_peer(o):
        return chip_peer(o // 2) + ((k + 1 - o % 2) % 2,)

    near = [device((x + o) % NX, y, z, k) for o in (2, 1, 3)]
    near += [device(x, (y + o) % NY, z, k) for o in (2, 1, 3)]
    near += [device(x, y, up, k), device(x, y, down, k), device(x, y, z, 1 - k)]
    for peer in near:
        pl.semaphore_signal(barrier, inc=1, device_id=peer, device_id_type=MESH)
    for (row, col), (at, flip) in TABLE.items():
        lookup[row * WIDTH + col - row + BAND - 1] = at * 2 + flip
    pl.semaphore_wait(barrier, len(near))

    def x_copy(direction, j):
        to = device((x + 1) % NX, y, z, k) if direction == 0 else device((x + NX - 1) % NX, y, z, k)
        first = (c if direction == 0 else 1 - c) * half + j * step
        return pltpu.make_async_remote_copy(
            src_ref=x_ref.at[pl.ds(first, step), :],
            dst_ref=cross.at[c, pl.ds(j * step, step), :],
            send_sem=x_send.at[direction, j],
            recv_sem=x_recv.at[c, j],
            device_id=to, device_id_type=MESH,
        )

    def x_arrival(side, j):
        return pltpu.make_async_remote_copy(
            src_ref=x_ref.at[pl.ds(0, step), :],
            dst_ref=cross.at[side, pl.ds(j * step, step), :],
            send_sem=x_send.at[0, j],
            recv_sem=x_recv.at[side, j],
            device_id=device((x + 1) % NX, y, z, k), device_id_type=MESH,
        )

    def forward(j):
        return pltpu.make_async_remote_copy(
            src_ref=cross.at[1, pl.ds(j * step, step), :],
            dst_ref=below.at[pl.ds(j * step, step), :],
            send_sem=zf_send.at[j], recv_sem=zf_recv.at[j],
            device_id=device(x, y, up, k), device_id_type=MESH,
        )

    for j in range(CHUNKS):
        x_copy(0, j).start()
        x_copy(1, j).start()
    edge = pltpu.make_async_remote_copy(
        src_ref=x_ref.at[:, pl.ds(0, BS)], dst_ref=ahead,
        send_sem=ze_send, recv_sem=ze_recv,
        device_id=device(x, y, down, k), device_id_type=MESH,
    )
    edge.start()
    share_pairs = pltpu.make_async_remote_copy(
        src_ref=pairs_ref, dst_ref=pairs_far, send_sem=pr_send, recv_sem=pr_recv,
        device_id=device((x + 2) % NX, y, z, k), device_id_type=MESH,
    )
    share_pairs.start()

    def swap(n, source, target):
        return pltpu.make_async_remote_copy(
            src_ref=source, dst_ref=target,
            send_sem=swap_send.at[n], recv_sem=swap_recv.at[n],
            device_id=device(x, y, z, 1 - k), device_id_type=MESH,
        )

    def strip(ref, block, core, *lead):
        first = pl.multiple_of(block * BS + core * (BS // 2), BS // 2)
        return ref.at[lead + (slice(None), pl.ds(first, BS // 2))]

    part = half // PARTS

    def swap_rows(g, i):
        rows = pl.ds(g * part, part)
        first = pl.multiple_of(i * BS + (1 - k) * (BS // 2), BS // 2)
        return swap(
            2 * g + i, cross.at[0, rows, pl.ds(first, BS // 2)],
            far_rows.at[rows, i * (BS // 2) : (i + 1) * (BS // 2)],
        )

    def swap_cols(g):
        rows = pl.ds(g * part, part)
        return swap(2 * PARTS + g, cross.at[1, rows, :], far_cols.at[rows, :])

    def swap_below(g):
        rows = pl.ds(g * part, part)
        return swap(3 * PARTS + g, below.at[rows, :], far_below.at[rows, :])

    swap_own = swap(4 * PARTS, strip(own, 1, 1 - k), far_own)
    swap_ahead = swap(4 * PARTS + 1, ahead, far_ahead)

    def put(ref, q, value):
        ref[..., q * 8 : q * 8 + 8, :] = value.reshape(ref.shape[:-2] + (8, BS))

    def to_sibling():
        return pltpu.make_async_remote_copy(
            src_ref=p_own.at[1 - k], dst_ref=k_own,
            send_sem=core_send, recv_sem=core_recv,
            device_id=device(x, y, z, 1 - k), device_id_type=MESH,
        )

    def scatter_copy(g, got, land, o):
        px, py = chip_peer(o)
        return pltpu.make_async_remote_copy(
            src_ref=got.at[py, px], dst_ref=land.at[me],
            send_sem=rs_send.at[g, o], recv_sem=rs_recv.at[g, me],
            device_id=device(px, py, z, k), device_id_type=MESH,
        )

    def scatter_arrival(g, got, land, o):
        px, py = chip_peer(o)
        source = py * NX + px
        return pltpu.make_async_remote_copy(
            src_ref=got.at[py, px], dst_ref=land.at[source],
            send_sem=rs_send.at[g, o], recv_sem=rs_recv.at[g, source],
            device_id=device(px, py, z, k), device_id_type=MESH,
        )

    def scatter(g, got, land):
        def send(o, carry):
            scatter_copy(g, got, land, o).start()
            return carry

        lax.fori_loop(0, CHIPS - 1, send, 0)
        land[me] = got[y, x]

    def collect(g, got, land):
        def take(o, carry):
            scatter_arrival(g, got, land, o).wait_recv()
            return carry

        lax.fori_loop(0, CHIPS - 1, take, 0)

    def y_copy(o, source):
        return pltpu.make_async_remote_copy(
            src_ref=k_own.at[(y + o) % NY], dst_ref=y_own.at[source],
            send_sem=y_send.at[o], recv_sem=y_recv.at[source],
            device_id=device(x, (y + o) % NY, z, k), device_id_type=MESH,
        )

    def row_copy(o, source):
        return pltpu.make_async_remote_copy(
            src_ref=s_own.at[(x + o) % NX], dst_ref=r_own.at[source],
            send_sem=row_send.at[o], recv_sem=row_recv.at[source],
            device_id=device((x + o) % NX, y, z, k), device_id_type=MESH,
        )

    def own_along_y():
        to_sibling().wait()
        for row in range(NY):
            k_own[row] = k_own[row] + p_own[k, row]
        for o in range(1, NY):
            y_copy(o, y).start()
        y_own[y] = k_own[y]

    def own_along_x():
        for o in range(1, NY):
            y_copy(o, (y + o) % NY).wait_recv()
        s_own[...] = (y_own[0] + y_own[1]) + (y_own[2] + y_own[3])
        for o in range(1, NX):
            row_copy(o, x).start()
        r_own[x] = s_own[x]

    load.wait()
    swap_own.start()
    put(p_own, 0, gram(own[:, :BS], own[:, :BS]))
    put(p_own, 1, gram(own[:, :BS], own[:, BS:]))
    put(p_own, 2, gram(own[:, BS:], own[:, BS:]))
    to_sibling().start()

    for j in range(CHUNKS):
        x_arrival(1, j).wait_recv()
        forward(j).start()
        x_arrival(0, j).wait_recv()
        if (j + 1) % (CHUNKS // PARTS) == 0:
            g = j // (CHUNKS // PARTS)
            swap_rows(g, 0).start()
            swap_rows(g, 1).start()
            swap_cols(g).start()
        if j == 0:
            own_along_y()
        if j == CHUNKS - 3:
            own_along_x()
    share_pairs.wait_recv()
    load_pairs.wait()
    far = pltpu.make_async_copy(pairs_far, pairs_all.at[1 - c], local_sem.at[2])
    far.start()

    for g in range(PARTS):
        swap_rows(g, 0).wait_recv()
        swap_rows(g, 1).wait_recv()
        swap_cols(g).wait_recv()

    near_rows = jnp.concatenate([strip(cross, 0, k, 0)[...], strip(cross, 1, k, 0)[...]], axis=1)

    def put_pairs(ref, near, far):
        for j in range(2):
            cols = slice(j * BS, (j + 1) * BS)
            both = gram(near_rows, near[:, cols]) + gram(far_rows[...], far[:, cols])
            put(ref, j, both[: BS // 2])
            put(ref, 2 + j, both[BS // 2 :])

    put_pairs(p_mid, cross.at[1], far_cols)

    def peak(ref, q):
        top = None
        for row in range(NY):
            for col in range(NX):
                size = jnp.abs(ref[row, col, q * 8 : q * 8 + 8, :])
                top = size if top is None else jnp.maximum(top, size)
        return jnp.max(top, axis=0, keepdims=True)

    rows = [exponents(peak(p_mid, q)) for q in range(4)]
    for q in range(4):
        scales[q : q + 1, :] = rows[q]
    shrink = spread([jnp.exp2(row * -0.125) for row in rows])
    for row in range(NY):
        for col in range(NX):
            q_mid[row, col] = to_i16(p_mid[row, col] * shrink)
    scatter(0, q_mid, r_mid)

    edge.wait_recv()
    swap_ahead.start()
    for g in range(PARTS):
        for j in range(g * CHUNKS // PARTS, (g + 1) * CHUNKS // PARTS):
            forward(j).wait_recv()
        swap_below(g).start()
    swap_own.wait_recv()
    swap_ahead.wait_recv()
    put(p_low, 4, gram(strip(own, 1, k)[...], ahead[...]) + gram(far_own[...], far_ahead[...]))
    for g in range(PARTS):
        swap_below(g).wait_recv()
    put_pairs(p_low, below, far_below)
    rows = [exponents(jnp.maximum(peak(p_low, q), peak(p_low, 2 + q))) for q in range(2)]
    rows.append(exponents(peak(p_low, 4)))
    for q in range(3):
        scales[4 + q : 5 + q, :] = rows[q]
    scales[7:8, :] = jnp.zeros((1, BS), jnp.float32)
    shrink = spread([jnp.exp2(rows[q] * -0.125) for q in (0, 1, 0, 1, 2)])
    for row in range(NY):
        for col in range(NX):
            q_low[row, col] = to_i16(jnp.concatenate([p_low[row, col] * shrink, scales[...]], axis=0))
    scatter(1, q_low, r_low)

    for o in range(1, NX):
        row_copy(o, (x + o) % NX).wait_recv()
    for side in range(2):
        table[3 * side : 3 * side + 3] = (r_own[2 * side] + r_own[2 * side + 1]).reshape(3, 8, BS)
    collect(1, q_low, r_low)
    edges, sums = [None, None], None
    for source in range(CHIPS):
        tail = to_f32(r_low[source, 32:48, :])
        grow[source] = jnp.exp2(tail[8:16, :] * 0.125)
        term = to_f32(r_low[source, 0:32, :]) * spread([grow[source, q : q + 1, :] for q in (4, 5, 4, 5)])
        sums = term if sums is None else sums + term
        edge_term = tail[0:8, :] * grow[source, 6:7, :]
        side = source % NX // 2
        edges[side] = edge_term if edges[side] is None else edges[side] + edge_term
    table[12:16] = sums.reshape(4, 8, BS)
    hop_down = pltpu.make_async_remote_copy(
        src_ref=table.at[pl.ds(12, 4)], dst_ref=table.at[pl.ds(16, 4)],
        send_sem=hop_send.at[1], recv_sem=hop_recv.at[1],
        device_id=device(x, y, down, k), device_id_type=MESH,
    )
    hop_down.start()
    table[6] = edges[0]
    table[7] = edges[1]
    hop_up = pltpu.make_async_remote_copy(
        src_ref=table.at[pl.ds(6, 2)], dst_ref=table.at[pl.ds(20, 2)],
        send_sem=hop_send.at[0], recv_sem=hop_recv.at[0],
        device_id=device(x, y, up, k), device_id_type=MESH,
    )
    hop_up.start()
    collect(0, q_mid, r_mid)
    sums = None
    for source in range(CHIPS):
        term = to_f32(r_mid[source]) * spread([grow[source, q : q + 1, :] for q in range(4)])
        sums = term if sums is None else sums + term
    table[8:12] = sums.reshape(4, 8, BS)
    def pack(first, count):
        value = table[first : first + count]
        scale = exponents(jnp.max(jnp.abs(value), axis=2, keepdims=True))
        packed[first : first + count, :, :BS] = value * jnp.exp2(scale * -0.125)
        packed[first : first + count, :, BS:] = jnp.broadcast_to(scale, (count, 8, 128))

    pack(0, 16)
    far.wait()
    hop_up.wait()
    hop_down.wait()
    pack(16, 6)

    def code(reader, slot):
        row = pairs_all[reader, 0, 0, slot]
        col = pairs_all[reader, 1, 0, slot]
        at = (row - z * BAND) * WIDTH + col - row + BAND - 1
        return lookup[jnp.clip(at, 0, BAND * WIDTH - 1)]

    def fill(o, px, py, pk):
        slot = 2 * (((px % 2) * NY + py) * 2 + pk)
        reader = px // 2
        both = [packed[code(reader, slot + s) // 2] for s in range(2)]
        stage[o] = to_i16(jnp.concatenate(both, axis=0))

    rank = k * CHIPS + me

    def deliver(o):
        px, py, pk = plane_peer(o)
        return pltpu.make_async_remote_copy(
            src_ref=stage.at[o], dst_ref=arrived.at[rank],
            send_sem=out_send.at[o], recv_sem=out_recv.at[rank],
            device_id=device(px, py, z, pk), device_id_type=MESH,
        )

    def send_out(o, carry):
        px, py, pk = plane_peer(o)
        fill(o, px, py, pk)
        deliver(o).start()
        return carry

    lax.fori_loop(0, 2 * CHIPS - 1, send_out, 0)
    fill(2 * CHIPS - 1, x, y, k)
    arrived[rank] = stage[2 * CHIPS - 1]

    def take_out(o, carry):
        px, py, pk = plane_peer(o)
        source = pk * CHIPS + py * NX + px
        pltpu.make_async_remote_copy(
            src_ref=stage.at[o], dst_ref=arrived.at[source],
            send_sem=out_send.at[o], recv_sem=out_recv.at[source],
            device_id=device(px, py, z, pk), device_id_type=MESH,
        ).wait_recv()
        return carry

    lax.fori_loop(0, 2 * CHIPS - 1, take_out, 0)
    def unpack(source, carry):
        value = to_f32(arrived[source])
        scale = jnp.exp2(value[:, BS:] * 0.125)
        value = value[:, :BS] * jnp.concatenate([scale, scale], axis=1)
        blocks[0, source] = value[:8]
        blocks[1, source] = value[8:]
        return carry

    lax.fori_loop(0, 2 * CHIPS, unpack, 0)
    for s in range(2):
        slot = 2 * token + s
        block = blocks[s].reshape(BS, BS)
        flip = code(c, slot) % 2 == 1
        block = jnp.where(flip, block.T, block)
        out_ref[0, s] = jnp.where(slot < counts_ref[0], block * weight, 0.0)

    for j in range(CHUNKS):
        x_copy(0, j).wait_send()
        x_copy(1, j).wait_send()
        forward(j).wait_send()
    for g in range(PARTS):
        swap_rows(g, 0).wait_send()
        swap_rows(g, 1).wait_send()
        swap_cols(g).wait_send()
        swap_below(g).wait_send()
    swap_own.wait_send()
    swap_ahead.wait_send()
    for o in range(1, NY):
        y_copy(o, y).wait_send()
    for o in range(1, NX):
        row_copy(o, x).wait_send()
    edge.wait_send()
    share_pairs.wait_send()
    for g, got, land in ((0, q_mid, r_mid), (1, q_low, r_low)):
        def left(o, carry):
            scatter_copy(g, got, land, o).wait_send()
            return carry

        lax.fori_loop(0, CHIPS - 1, left, 0)

    def left_out(o, carry):
        deliver(o).wait_send()
        return carry

    lax.fori_loop(0, 2 * CHIPS - 1, left_out, 0)


def shards(layer_input, pairs, counts):
    rows, columns = layer_input.shape
    weight = 2.0 / (rows * lax.axis_size("token"))
    dma, vmem = pltpu.SemaphoreType.DMA, pltpu.VMEM
    f32, bf16, i16 = jnp.float32, jnp.bfloat16, jnp.int16
    slots = pairs.shape[2] // lax.axis_size("token")
    scratch = [
        vmem((rows, columns), bf16),
        vmem((2, rows // 2, columns), bf16),
        vmem((rows // 2, columns), bf16),
        vmem((rows, BS), bf16),
    ]
    scratch += [
        vmem((rows // 2, BS), bf16),
        vmem((rows // 2, columns), bf16),
        vmem((rows // 2, columns), bf16),
        vmem((rows, BS // 2), bf16),
        vmem((rows, BS), bf16),
        vmem((2, NY, NX, 24, BS), f32), vmem((NY, NX, 24, BS), f32),
        vmem((NY, NX, 32, BS), f32), vmem((NY, NX, 40, BS), f32),
        vmem((NY, NX, 32, BS), i16), vmem((NY, NX, 48, BS), i16), vmem((8, BS), f32),
        vmem((NX, 24, BS), f32), vmem((CHIPS, 32, BS), i16), vmem((CHIPS, 48, BS), i16),
        vmem((CHIPS, 8, BS), f32),
    ]
    scratch += [
        vmem((22, 8, BS), f32),
        vmem((22, 8, BS + 128), f32),
        vmem((slots, 2 * CHIPS, 8, BS), f32),
        vmem((2 * CHIPS, 8 * slots, BS + 128), i16),
        vmem((2 * CHIPS, 8 * slots, BS + 128), i16),
        vmem(pairs.shape, jnp.int32),
        pltpu.SMEM((2,) + pairs.shape, jnp.int32),
        pltpu.SMEM((BAND * WIDTH,), jnp.int32),
        dma((3,)),
        dma((2, CHUNKS)), dma((2, CHUNKS)),
        dma((CHUNKS,)), dma((CHUNKS,)),
        dma, dma, dma, dma,
        dma, dma, dma((4 * PARTS + 2,)), dma((4 * PARTS + 2,)),
        vmem((NY, NX, 24, BS), f32), vmem((NX, 24, BS), f32),
        dma((NY,)), dma((NY,)), dma((NX,)), dma((NX,)),
        dma((2, CHIPS)), dma((2, CHIPS)),
        dma((2,)), dma((2,)),
        dma((2 * CHIPS,)), dma((2 * CHIPS,)),
    ]
    return pl.pallas_call(
        functools.partial(kernel, weight),
        out_shape=jax.ShapeDtypeStruct((1, slots, BS, BS), f32),
        in_specs=[
            pl.BlockSpec(memory_space=pltpu.HBM),
            pl.BlockSpec(memory_space=pltpu.HBM),
            pl.BlockSpec(memory_space=pltpu.SMEM),
        ],
        out_specs=pl.BlockSpec(memory_space=pltpu.VMEM),
        scratch_shapes=scratch,
        compiler_params=pltpu.CompilerParams(
            collective_id=0, has_side_effects=True, vmem_limit_bytes=211 * 2**18
        ),
    )(layer_input, pairs, counts)


def solution(mesh):
    return jax.shard_map(
        shards,
        mesh=mesh,
        in_specs=(
            P("token", ("brow", "bcol")),
            P(None, ("brow", "bcol"), None),
            P(("brow", "bcol")),
        ),
        out_specs=P(("brow", "bcol"), "token", None, None),
        check_vma=False,
    )
```

```python
import functools
import jax
import jax.numpy as jnp
from jax import lax
from jax.experimental import pallas as pl
from jax.experimental.pallas import tpu as pltpu
from jax.sharding import PartitionSpec as P

BS = 256
BAND = 4
NX, NY, NZ = 4, 4, 8
CHIPS = NX * NY
CHUNKS = 8
PARTS = 4
FULL = 32000.0
MESH = pl.DeviceIdType.MESH

TABLE = {
    (0, 0): (0, 0), (0, 1): (1, 0), (1, 1): (2, 0),
    (2, 2): (3, 0), (2, 3): (4, 0), (3, 3): (5, 0),
    (1, 4): (6, 0), (3, 6): (7, 0),
    (0, 2): (8, 0), (0, 3): (9, 0), (1, 2): (10, 0), (1, 3): (11, 0),
    (0, -2): (12, 0), (0, -1): (13, 0), (1, -2): (14, 0), (1, -1): (15, 0),
    (2, 4): (16, 1), (3, 4): (17, 1), (2, 5): (18, 1), (3, 5): (19, 1),
    (0, -3): (20, 1), (2, -1): (21, 1),
    (1, 0): (1, 1), (3, 2): (4, 1),
    (2, 0): (8, 1), (3, 0): (9, 1), (2, 1): (10, 1), (3, 1): (11, 1),
}
WIDTH = 2 * BAND - 1


def device(x, y, z, k):
    return (((x % 2) * NY + y) * 2 + k, z, x // 2)


def gram(a, b):
    return lax.dot_general(a, b, (((0,), (0,)), ((), ())), preferred_element_type=jnp.float32)


def far_first(n):
    return (2 + 3 * n + 3 * (n * (n - 1) // 2)) % 4


def exponents(peak):
    return jnp.ceil(8.0 * jnp.log2(jnp.maximum(peak, 1e-30)))


def spread(rows):
    return jnp.concatenate([jnp.broadcast_to(row, (8, row.shape[1])) for row in rows], axis=0)


def compress(value):
    root = FULL * jnp.sqrt(jnp.abs(value))
    return jnp.where(value < 0.0, -root, root)


def expand(coded):
    return coded * jnp.abs(coded) * (1.0 / (FULL * FULL))


def to_i16(value):
    return jnp.floor(value + 0.5).astype(jnp.int32).astype(jnp.int16)


def to_f32(value):
    return value.astype(jnp.int32).astype(jnp.float32)


def kernel(
    weight, x_ref, pairs_ref, counts_ref, out_ref,
    own, cross, below, ahead, far_rows, far_cols, far_below,
    p_own, k_own, rows_t, sums_low, p_mid, p_low, p_edge, k_edge, q_mid, q_low, q_edge, scales, scales_low, r_own, r_mid, r_low, r_edge, grow, factor, table, packed, blocks, stage, arrived, pairs_far, pairs_all, lookup, codes,
    local_sem, x_send, x_recv, zf_send, zf_recv, ze_send, ze_recv, pr_send, pr_recv,
    core_send, core_recv, swap_send, swap_recv, y_own, s_own, y_send, y_recv, row_send, row_recv, rs_send, rs_recv, hop_send, hop_recv, out_send, out_recv,
):
    token = lax.axis_index("token")
    z = lax.axis_index("brow")
    c = lax.axis_index("bcol")
    k = token % 2
    y = (token // 2) % NY
    x = 2 * c + token // (2 * NY)
    me = y * NX + x
    half = x_ref.shape[0] // 2
    step = half // CHUNKS
    up, down = (z + 1) % NZ, (z + NZ - 1) % NZ

    load = pltpu.make_async_copy(x_ref, own, local_sem.at[0])
    load.start()
    load_pairs = pltpu.make_async_copy(pairs_ref, pairs_all.at[c], local_sem.at[1])
    load_pairs.start()

    barrier = pltpu.get_barrier_semaphore()

    def chip_peer(o):
        return (x + far_first(o % NX)) % NX, (y + far_first(o // NX)) % NY

    def plane_peer(o):
        return chip_peer(o // 2) + ((k + 1 - o % 2) % 2,)

    near = [device((x + o) % NX, y, z, k) for o in (2, 1, 3)]
    near += [device(x, (y + o) % NY, z, k) for o in (2, 1, 3)]
    near += [device(x, y, up, k), device(x, y, down, k), device(x, y, z, 1 - k)]
    for peer in near:
        pl.semaphore_signal(barrier, inc=1, device_id=peer, device_id_type=MESH)
    for (row, col), (at, flip) in TABLE.items():
        lookup[row * WIDTH + col - row + BAND - 1] = at * 2 + flip
    pl.semaphore_wait(barrier, len(near))

    def x_copy(direction, j):
        to = device((x + 1) % NX, y, z, k) if direction == 0 else device((x + NX - 1) % NX, y, z, k)
        first = (c if direction == 0 else 1 - c) * half + j * step
        return pltpu.make_async_remote_copy(
            src_ref=x_ref.at[pl.ds(first, step), :],
            dst_ref=cross.at[c, pl.ds(j * step, step), :],
            send_sem=x_send.at[direction, j],
            recv_sem=x_recv.at[c, j],
            device_id=to, device_id_type=MESH,
        )

    def x_arrival(side, j):
        return pltpu.make_async_remote_copy(
            src_ref=x_ref.at[pl.ds(0, step), :],
            dst_ref=cross.at[side, pl.ds(j * step, step), :],
            send_sem=x_send.at[0, j],
            recv_sem=x_recv.at[side, j],
            device_id=device((x + 1) % NX, y, z, k), device_id_type=MESH,
        )

    def forward(j):
        return pltpu.make_async_remote_copy(
            src_ref=cross.at[1, pl.ds(j * step, step), :],
            dst_ref=below.at[pl.ds(j * step, step), :],
            send_sem=zf_send.at[j], recv_sem=zf_recv.at[j],
            device_id=device(x, y, up, k), device_id_type=MESH,
        )

    for j in range(CHUNKS):
        x_copy(0, j).start()
        x_copy(1, j).start()
    edge = pltpu.make_async_remote_copy(
        src_ref=x_ref.at[:, pl.ds(0, BS)], dst_ref=ahead,
        send_sem=ze_send, recv_sem=ze_recv,
        device_id=device(x, y, down, k), device_id_type=MESH,
    )
    edge.start()
    share_pairs = pltpu.make_async_remote_copy(
        src_ref=pairs_ref, dst_ref=pairs_far, send_sem=pr_send, recv_sem=pr_recv,
        device_id=device((x + 2) % NX, y, z, k), device_id_type=MESH,
    )
    share_pairs.start()

    def swap(n, source, target):
        return pltpu.make_async_remote_copy(
            src_ref=source, dst_ref=target,
            send_sem=swap_send.at[n], recv_sem=swap_recv.at[n],
            device_id=device(x, y, z, 1 - k), device_id_type=MESH,
        )

    part = half // PARTS

    def swap_rows(g, i):
        rows = pl.ds(g * part, part)
        first = pl.multiple_of(i * BS + (1 - k) * (BS // 2), BS // 2)
        return swap(
            2 * g + i, cross.at[0, rows, pl.ds(first, BS // 2)],
            far_rows.at[rows, i * (BS // 2) : (i + 1) * (BS // 2)],
        )

    def swap_cols(g):
        rows = pl.ds(g * part, part)
        return swap(2 * PARTS + g, cross.at[1, rows, :], far_cols.at[rows, :])

    def swap_below(g):
        rows = pl.ds(g * part, part)
        return swap(3 * PARTS + g, below.at[rows, :], far_below.at[rows, :])

    def put(ref, q, value):
        ref[..., q * 8 : q * 8 + 8, :] = value.reshape(ref.shape[:-2] + (8, BS))

    def to_sibling(n, ref, got):
        return pltpu.make_async_remote_copy(
            src_ref=ref.at[1 - k], dst_ref=got,
            send_sem=core_send.at[n], recv_sem=core_recv.at[n],
            device_id=device(x, y, z, 1 - k), device_id_type=MESH,
        )

    def scatter_copy(g, got, land, o):
        px, py = chip_peer(o)
        return pltpu.make_async_remote_copy(
            src_ref=got.at[py, px], dst_ref=land.at[me],
            send_sem=rs_send.at[g, o], recv_sem=rs_recv.at[g, me],
            device_id=device(px, py, z, k), device_id_type=MESH,
        )

    def scatter_arrival(g, got, land, o):
        px, py = chip_peer(o)
        source = py * NX + px
        return pltpu.make_async_remote_copy(
            src_ref=got.at[py, px], dst_ref=land.at[source],
            send_sem=rs_send.at[g, o], recv_sem=rs_recv.at[g, source],
            device_id=device(px, py, z, k), device_id_type=MESH,
        )

    def scatter(g, encode, got, land):
        def send(o, carry):
            px, py = chip_peer(o)
            got[py, px] = encode(py, px)
            scatter_copy(g, got, land, o).start()
            return carry

        lax.fori_loop(0, CHIPS - 1, send, 0)
        land[me] = encode(y, x)

    def collect(g, got, land):
        def take(o, carry):
            scatter_arrival(g, got, land, o).wait_recv()
            return carry

        lax.fori_loop(0, CHIPS - 1, take, 0)

    def y_copy(o, source):
        return pltpu.make_async_remote_copy(
            src_ref=k_own.at[(y + o) % NY], dst_ref=y_own.at[source],
            send_sem=y_send.at[o], recv_sem=y_recv.at[source],
            device_id=device(x, (y + o) % NY, z, k), device_id_type=MESH,
        )

    def row_copy(o, source):
        return pltpu.make_async_remote_copy(
            src_ref=s_own.at[(x + o) % NX], dst_ref=r_own.at[source],
            send_sem=row_send.at[o], recv_sem=row_recv.at[source],
            device_id=device((x + o) % NX, y, z, k), device_id_type=MESH,
        )

    def own_along_y():
        to_sibling(0, p_own, k_own).wait()
        for row in range(NY):
            k_own[row] = k_own[row] + p_own[k, row]
        for o in range(1, NY):
            y_copy(o, y).start()
        y_own[y] = k_own[y]

    def own_along_x():
        for o in range(1, NY):
            y_copy(o, (y + o) % NY).wait_recv()
        s_own[...] = (y_own[0] + y_own[1]) + (y_own[2] + y_own[3])
        for o in range(1, NX):
            row_copy(o, x).start()
        r_own[x] = s_own[x]

    load.wait()
    put(p_own, 0, gram(own[:, :BS], own[:, :BS]))
    put(p_own, 1, gram(own[:, :BS], own[:, BS:]))
    put(p_own, 2, gram(own[:, BS:], own[:, BS:]))
    to_sibling(0, p_own, k_own).start()

    per_part = CHUNKS // PARTS

    def pass_below(g):
        for j in range(g * per_part, (g + 1) * per_part):
            forward(j).wait_recv()
        swap_below(g).start()

    for j in range(CHUNKS):
        x_arrival(1, j).wait_recv()
        forward(j).start()
        x_arrival(0, j).wait_recv()
        if j == 0:
            own_along_y()
        if (j + 1) % per_part == 0:
            g = j // per_part
            swap_rows(g, 0).start()
            swap_rows(g, 1).start()
            swap_cols(g).start()
            tokens = slice(g * part, (g + 1) * part)
            near = [cross[0, tokens, pl.ds(pl.multiple_of(i * BS + k * (BS // 2), BS // 2), BS // 2)] for i in range(2)]
            rows_t[:, tokens] = jnp.concatenate(near, axis=1).T
            if g >= 2:
                pass_below(g - 2)
    share_pairs.wait_recv()
    load_pairs.wait()
    far = pltpu.make_async_copy(pairs_far, pairs_all.at[1 - c], local_sem.at[2])
    far.start()

    for g in range(PARTS):
        swap_rows(g, 0).wait_recv()
        swap_rows(g, 1).wait_recv()
        rows_t[:, half + g * part : half + (g + 1) * part] = far_rows[g * part : (g + 1) * part, :].T
        swap_cols(g).wait_recv()

    def product(near, far_part, first, last, cols):
        return jnp.dot(
            rows_t[:, first:last], near[first:last, cols], preferred_element_type=jnp.float32
        ) + jnp.dot(
            rows_t[:, half + first : half + last], far_part[first:last, cols], preferred_element_type=jnp.float32
        )

    def put_pairs(ref, j, both):
        put(ref, j, both[: BS // 2])
        put(ref, 2 + j, both[BS // 2 :])

    def peak(ref, q):
        top = None
        for row in range(NY):
            for col in range(NX):
                size = jnp.abs(ref[row, col, q * 8 : q * 8 + 8, :])
                top = size if top is None else jnp.maximum(top, size)
        return jnp.max(top, axis=0, keepdims=True)

    for j in range(2):
        put_pairs(p_mid, j, product(cross.at[1], far_cols, 0, half, slice(j * BS, (j + 1) * BS)))
    rows = [exponents(peak(p_mid, q)) for q in range(4)]
    scales[...] = jnp.zeros_like(scales)
    for q in range(4):
        scales[q : q + 1, :] = rows[q]
    grow[0:32, :] = spread([jnp.exp2(row * -0.125) for row in rows])
    scatter(0, lambda row, col: to_i16(compress(p_mid[row, col] * grow[0:32, :])), q_mid, r_mid)

    pass_below(PARTS - 2)
    edge.wait_recv()
    put(p_edge, 0, gram(own[:, BS:], ahead[...]))
    to_sibling(1, p_edge, k_edge).start()
    own_along_x()
    early = half - part
    for g in range(PARTS - 1):
        swap_below(g).wait_recv()
    for j in range(2):
        cols = slice(j * BS, (j + 1) * BS)
        sums_low[:, cols] = product(below, far_below, 0, early, cols)
    to_sibling(1, p_edge, k_edge).wait()
    k_edge[...] = k_edge[...] + p_edge[k]
    row = exponents(peak(k_edge, 0))
    scales[4:5, :] = row
    grow[32:40, :] = spread([jnp.exp2(row * -0.125)])

    def encode_edge(row, col):
        coded = compress(k_edge[row, col] * grow[32:40, :])
        return to_i16(jnp.concatenate([coded, scales[...]], axis=0))

    scatter(2, encode_edge, q_edge, r_edge)
    pass_below(PARTS - 1)
    swap_below(PARTS - 1).wait_recv()
    for j in range(2):
        cols = slice(j * BS, (j + 1) * BS)
        put_pairs(p_low, j, sums_low[:, cols] + product(below, far_below, early, half, cols))
    rows = [exponents(jnp.maximum(peak(p_low, q), peak(p_low, 2 + q))) for q in range(2)]
    scales_low[...] = jnp.zeros_like(scales_low)
    for q in range(2):
        for h in range(2):
            scales_low[2 * q + h : 2 * q + h + 1, :] = rows[q][:, h * 128 : h * 128 + 128]
    grow[40:72, :] = spread([jnp.exp2(rows[q] * -0.125) for q in (0, 1, 0, 1)])

    def encode_low(row, col):
        coded = compress(p_low[row, col] * grow[40:72, :])
        return to_i16(jnp.concatenate([coded[:, :128], coded[:, 128:], scales_low[...]], axis=0))

    scatter(1, encode_low, q_low, r_low)

    far.wait()

    def code(reader, slot):
        row = pairs_all[reader, 0, 0, slot]
        col = pairs_all[reader, 1, 0, slot]
        at = (row - z * BAND) * WIDTH + col - row + BAND - 1
        return lookup[jnp.clip(at, 0, BAND * WIDTH - 1)]

    def note(o, carry):
        px, py, pk = plane_peer(o)
        slot = 2 * (((px % 2) * NY + py) * 2 + pk)
        for s in range(2):
            codes[2 * o + s] = code(px // 2, slot + s)
        return carry

    lax.fori_loop(0, 2 * CHIPS, note, 0)

    for o in range(1, NX):
        row_copy(o, (x + o) % NX).wait_recv()
    for side in range(2):
        table[3 * side : 3 * side + 3] = (r_own[2 * side] + r_own[2 * side + 1]).reshape(3, 8, BS)
    def pack(first, count):
        value = table[first : first + count]
        scale = exponents(jnp.max(jnp.abs(value), axis=2, keepdims=True))
        packed[first : first + count, :, :BS] = compress(value * jnp.exp2(scale * -0.125))
        packed[first : first + count, :, BS:] = jnp.broadcast_to(scale, (count, 8, 128))

    collect(2, q_edge, r_edge)
    edges = [None, None]
    for source in range(CHIPS):
        tail = to_f32(r_edge[source])
        factor[source] = jnp.exp2(tail[8:16, :] * 0.125)
        term = expand(tail[0:8, :]) * factor[source, 4:5, :]
        side = source % NX // 2
        edges[side] = term if edges[side] is None else edges[side] + term
    table[6] = edges[0]
    table[7] = edges[1]
    hop_up = pltpu.make_async_remote_copy(
        src_ref=table.at[pl.ds(6, 2)], dst_ref=table.at[pl.ds(20, 2)],
        send_sem=hop_send.at[0], recv_sem=hop_recv.at[0],
        device_id=device(x, y, up, k), device_id_type=MESH,
    )
    hop_up.start()
    collect(0, q_mid, r_mid)
    sums = None
    for source in range(CHIPS):
        term = expand(to_f32(r_mid[source])) * spread([factor[source, q : q + 1, :] for q in range(4)])
        sums = term if sums is None else sums + term
    table[8:12] = sums.reshape(4, 8, BS)
    pack(0, 12)

    collect(1, q_low, r_low)
    sums = [None, None]
    for source in range(CHIPS):
        coded = to_f32(r_low[source])
        scale = jnp.exp2(coded[64:80, :] * 0.125)
        for h in range(2):
            term = expand(coded[32 * h : 32 * h + 32, :]) * spread(
                [scale[2 * q + h : 2 * q + h + 1, :] for q in (0, 1, 0, 1)]
            )
            sums[h] = term if sums[h] is None else sums[h] + term
    table[12:16] = jnp.concatenate(sums, axis=1).reshape(4, 8, BS)
    hop_down = pltpu.make_async_remote_copy(
        src_ref=table.at[pl.ds(12, 4)], dst_ref=table.at[pl.ds(16, 4)],
        send_sem=hop_send.at[1], recv_sem=hop_recv.at[1],
        device_id=device(x, y, down, k), device_id_type=MESH,
    )
    hop_down.start()
    pack(12, 4)
    hop_up.wait()
    pack(20, 2)
    hop_down.wait()
    pack(16, 4)

    def fill(o):
        both = [packed[codes[2 * o + s] // 2] for s in range(2)]
        stage[o] = to_i16(jnp.concatenate(both, axis=0))

    rank = k * CHIPS + me

    def deliver(o):
        px, py, pk = plane_peer(o)
        return pltpu.make_async_remote_copy(
            src_ref=stage.at[o], dst_ref=arrived.at[rank],
            send_sem=out_send.at[o], recv_sem=out_recv.at[rank],
            device_id=device(px, py, z, pk), device_id_type=MESH,
        )

    def send_out(o, carry):
        fill(o)
        deliver(o).start()
        return carry

    lax.fori_loop(0, 2 * CHIPS - 1, send_out, 0)
    fill(2 * CHIPS - 1)
    arrived[rank] = stage[2 * CHIPS - 1]

    for j in range(CHUNKS):
        x_copy(0, j).wait_send()
        x_copy(1, j).wait_send()
        forward(j).wait_send()
    for g in range(PARTS):
        swap_rows(g, 0).wait_send()
        swap_rows(g, 1).wait_send()
        swap_cols(g).wait_send()
        swap_below(g).wait_send()
    for o in range(1, NY):
        y_copy(o, y).wait_send()
    for o in range(1, NX):
        row_copy(o, x).wait_send()
    edge.wait_send()
    share_pairs.wait_send()
    for g, got, land in ((0, q_mid, r_mid), (1, q_low, r_low), (2, q_edge, r_edge)):
        def left(o, carry):
            scatter_copy(g, got, land, o).wait_send()
            return carry

        lax.fori_loop(0, CHIPS - 1, left, 0)

    def left_out(o, carry):
        deliver(o).wait_send()
        return carry

    lax.fori_loop(0, 2 * CHIPS - 1, left_out, 0)

    def unpack(source):
        value = to_f32(arrived[source])
        scale = jnp.exp2(value[:, BS:] * 0.125)
        value = expand(value[:, :BS]) * jnp.concatenate([scale, scale], axis=1)
        blocks[0, source] = value[:8]
        blocks[1, source] = value[8:]

    unpack(rank)

    def take_out(o, carry):
        px, py, pk = plane_peer(o)
        source = pk * CHIPS + py * NX + px
        pltpu.make_async_remote_copy(
            src_ref=stage.at[o], dst_ref=arrived.at[source],
            send_sem=out_send.at[o], recv_sem=out_recv.at[source],
            device_id=device(px, py, z, pk), device_id_type=MESH,
        ).wait_recv()
        unpack(source)
        return carry

    lax.fori_loop(0, 2 * CHIPS - 1, take_out, 0)
    for s in range(2):
        slot = 2 * token + s
        block = blocks[s].reshape(BS, BS)
        flip = code(c, slot) % 2 == 1
        block = jnp.where(flip, block.T, block)
        out_ref[0, s] = jnp.where(slot < counts_ref[0], block * weight, 0.0)


def shards(layer_input, pairs, counts):
    rows, columns = layer_input.shape
    weight = 2.0 / (rows * lax.axis_size("token"))
    dma, vmem = pltpu.SemaphoreType.DMA, pltpu.VMEM
    f32, bf16, i16 = jnp.float32, jnp.bfloat16, jnp.int16
    slots = pairs.shape[2] // lax.axis_size("token")
    scratch = [
        vmem((rows, columns), bf16),
        vmem((2, rows // 2, columns), bf16),
        vmem((rows // 2, columns), bf16),
        vmem((rows, BS), bf16),
    ]
    scratch += [
        vmem((rows // 2, BS), bf16),
        vmem((rows // 2, columns), bf16),
        vmem((rows // 2, columns), bf16),
        vmem((2, NY, NX, 24, BS), f32), vmem((NY, NX, 24, BS), f32),
        vmem((BS, rows), bf16), vmem((BS, columns), f32),
        vmem((NY, NX, 32, BS), f32), vmem((NY, NX, 32, BS), f32),
        vmem((2, NY, NX, 8, BS), f32), vmem((NY, NX, 8, BS), f32),
        vmem((NY, NX, 32, BS), i16), vmem((NY, NX, 80, 128), i16), vmem((NY, NX, 16, BS), i16),
        vmem((8, BS), f32), vmem((16, 128), f32), vmem((NX, 24, BS), f32),
        vmem((CHIPS, 32, BS), i16), vmem((CHIPS, 80, 128), i16), vmem((CHIPS, 16, BS), i16),
        vmem((72, BS), f32), vmem((CHIPS, 8, BS), f32),
    ]
    scratch += [
        vmem((22, 8, BS), f32),
        vmem((22, 8, BS + 128), f32),
        vmem((slots, 2 * CHIPS, 8, BS), f32),
        vmem((2 * CHIPS, 8 * slots, BS + 128), i16),
        vmem((2 * CHIPS, 8 * slots, BS + 128), i16),
        vmem(pairs.shape, jnp.int32),
        pltpu.SMEM((2,) + pairs.shape, jnp.int32),
        pltpu.SMEM((BAND * WIDTH,), jnp.int32),
        pltpu.SMEM((4 * CHIPS,), jnp.int32),
        dma((3,)),
        dma((2, CHUNKS)), dma((2, CHUNKS)),
        dma((CHUNKS,)), dma((CHUNKS,)),
        dma, dma, dma, dma,
        dma((2,)), dma((2,)), dma((4 * PARTS,)), dma((4 * PARTS,)),
        vmem((NY, NX, 24, BS), f32), vmem((NX, 24, BS), f32),
        dma((NY,)), dma((NY,)), dma((NX,)), dma((NX,)),
        dma((3, CHIPS)), dma((3, CHIPS)),
        dma((2,)), dma((2,)),
        dma((2 * CHIPS,)), dma((2 * CHIPS,)),
    ]
    return pl.pallas_call(
        functools.partial(kernel, weight),
        out_shape=jax.ShapeDtypeStruct((1, slots, BS, BS), f32),
        in_specs=[
            pl.BlockSpec(memory_space=pltpu.HBM),
            pl.BlockSpec(memory_space=pltpu.HBM),
            pl.BlockSpec(memory_space=pltpu.SMEM),
        ],
        out_specs=pl.BlockSpec(memory_space=pltpu.VMEM),
        scratch_shapes=scratch,
        compiler_params=pltpu.CompilerParams(
            collective_id=0, has_side_effects=True, vmem_limit_bytes=211 * 2**18
        ),
    )(layer_input, pairs, counts)


def solution(mesh):
    return jax.shard_map(
        shards,
        mesh=mesh,
        in_specs=(
            P("token", ("brow", "bcol")),
            P(None, ("brow", "bcol"), None),
            P(("brow", "bcol")),
        ),
        out_specs=P(("brow", "bcol"), "token", None, None),
        check_vma=False,
    )
```

```python
import functools
import jax
import jax.numpy as jnp
from jax import lax
from jax.experimental import pallas as pl
from jax.experimental.pallas import tpu as pltpu
from jax.sharding import PartitionSpec as P

BS = 256
BAND = 4
NX, NY, NZ = 4, 4, 8
CHIPS = NX * NY
CHUNKS = 8
PARTS = 4
FULL = 32000.0
MESH = pl.DeviceIdType.MESH

TABLE = {
    (0, 0): (0, 0), (0, 1): (1, 0), (1, 1): (2, 0),
    (2, 2): (3, 0), (2, 3): (4, 0), (3, 3): (5, 0),
    (1, 4): (6, 0), (3, 6): (7, 0),
    (0, 2): (8, 0), (0, 3): (9, 0), (1, 2): (10, 0), (1, 3): (11, 0),
    (0, -2): (12, 0), (0, -1): (13, 0), (1, -2): (14, 0), (1, -1): (15, 0),
    (2, 4): (16, 1), (3, 4): (17, 1), (2, 5): (18, 1), (3, 5): (19, 1),
    (0, -3): (20, 1), (2, -1): (21, 1),
    (1, 0): (1, 1), (3, 2): (4, 1),
    (2, 0): (8, 1), (3, 0): (9, 1), (2, 1): (10, 1), (3, 1): (11, 1),
}
WIDTH = 2 * BAND - 1


def device(x, y, z, k):
    return (((x % 2) * NY + y) * 2 + k, z, x // 2)


def gram(a, b):
    return lax.dot_general(a, b, (((0,), (0,)), ((), ())), preferred_element_type=jnp.float32)


def far_first(n):
    return (2 + 3 * n + 3 * (n * (n - 1) // 2)) % 4


def exponents(peak):
    return jnp.ceil(8.0 * jnp.log2(jnp.maximum(peak, 1e-30)))


def spread(rows):
    return jnp.concatenate([jnp.broadcast_to(row, (8, row.shape[1])) for row in rows], axis=0)


def compress(value):
    root = FULL * jnp.sqrt(jnp.abs(value))
    return jnp.where(value < 0.0, -root, root)


def expand(coded):
    return coded * jnp.abs(coded) * (1.0 / (FULL * FULL))


def to_i16(value):
    return jnp.floor(value + 0.5).astype(jnp.int32).astype(jnp.int16)


def to_f32(value):
    return value.astype(jnp.int32).astype(jnp.float32)


def kernel(
    weight, x_ref, pairs_ref, counts_ref, out_ref,
    own, cross, below, ahead, far_rows, far_cols, far_below,
    p_own, k_own, rows_t, sums_low, p_mid, p_low, p_edge, k_edge, q_mid, q_low, q_edge, scales, scales_low, r_own, r_mid, r_low, r_edge, grow, factor, table, packed, blocks, stage, arrived, pairs_far, pairs_all, lookup, codes,
    local_sem, x_send, x_recv, zf_send, zf_recv, ze_send, ze_recv, pr_send, pr_recv,
    core_send, core_recv, swap_send, swap_recv, y_own, s_own, y_send, y_recv, row_send, row_recv, rs_send, rs_recv, hop_send, hop_recv, out_send, out_recv,
):
    token = lax.axis_index("token")
    z = lax.axis_index("brow")
    c = lax.axis_index("bcol")
    k = token % 2
    y = (token // 2) % NY
    x = 2 * c + token // (2 * NY)
    me = y * NX + x
    half = x_ref.shape[0] // 2
    step = half // CHUNKS
    up, down = (z + 1) % NZ, (z + NZ - 1) % NZ

    load = pltpu.make_async_copy(x_ref, own, local_sem.at[0])
    load.start()
    load_pairs = pltpu.make_async_copy(pairs_ref, pairs_all.at[c], local_sem.at[1])
    load_pairs.start()

    barrier = pltpu.get_barrier_semaphore()

    def chip_peer(o):
        return (x + far_first(o % NX)) % NX, (y + far_first(o // NX)) % NY

    def plane_peer(o):
        return chip_peer(o // 2) + ((k + 1 - o % 2) % 2,)

    near = [device((x + o) % NX, y, z, k) for o in (2, 1, 3)]
    near += [device(x, (y + o) % NY, z, k) for o in (2, 1, 3)]
    near += [device(x, y, up, k), device(x, y, down, k), device(x, y, z, 1 - k)]
    for peer in near:
        pl.semaphore_signal(barrier, inc=1, device_id=peer, device_id_type=MESH)
    for (row, col), (at, flip) in TABLE.items():
        lookup[row * WIDTH + col - row + BAND - 1] = at * 2 + flip
    pl.semaphore_wait(barrier, len(near))

    def x_copy(direction, j):
        to = device((x + 1) % NX, y, z, k) if direction == 0 else device((x + NX - 1) % NX, y, z, k)
        first = (c if direction == 0 else 1 - c) * half + j * step
        return pltpu.make_async_remote_copy(
            src_ref=x_ref.at[pl.ds(first, step), :],
            dst_ref=cross.at[c, pl.ds(j * step, step), :],
            send_sem=x_send.at[direction, j],
            recv_sem=x_recv.at[c, j],
            device_id=to, device_id_type=MESH,
        )

    def x_arrival(side, j):
        return pltpu.make_async_remote_copy(
            src_ref=x_ref.at[pl.ds(0, step), :],
            dst_ref=cross.at[side, pl.ds(j * step, step), :],
            send_sem=x_send.at[0, j],
            recv_sem=x_recv.at[side, j],
            device_id=device((x + 1) % NX, y, z, k), device_id_type=MESH,
        )

    def forward(j):
        return pltpu.make_async_remote_copy(
            src_ref=cross.at[1, pl.ds(j * step, step), :],
            dst_ref=below.at[pl.ds(j * step, step), :],
            send_sem=zf_send.at[j], recv_sem=zf_recv.at[j],
            device_id=device(x, y, up, k), device_id_type=MESH,
        )

    for j in range(CHUNKS):
        x_copy(0, j).start()
        x_copy(1, j).start()
    edge = pltpu.make_async_remote_copy(
        src_ref=x_ref.at[:, pl.ds(0, BS)], dst_ref=ahead,
        send_sem=ze_send, recv_sem=ze_recv,
        device_id=device(x, y, down, k), device_id_type=MESH,
    )
    edge.start()
    share_pairs = pltpu.make_async_remote_copy(
        src_ref=pairs_ref, dst_ref=pairs_far, send_sem=pr_send, recv_sem=pr_recv,
        device_id=device((x + 2) % NX, y, z, k), device_id_type=MESH,
    )
    share_pairs.start()

    def swap(n, source, target):
        return pltpu.make_async_remote_copy(
            src_ref=source, dst_ref=target,
            send_sem=swap_send.at[n], recv_sem=swap_recv.at[n],
            device_id=device(x, y, z, 1 - k), device_id_type=MESH,
        )

    part = half // PARTS

    def swap_rows(g, i):
        rows = pl.ds(g * part, part)
        first = pl.multiple_of(i * BS + (1 - k) * (BS // 2), BS // 2)
        return swap(
            2 * g + i, cross.at[0, rows, pl.ds(first, BS // 2)],
            far_rows.at[rows, i * (BS // 2) : (i + 1) * (BS // 2)],
        )

    def swap_cols(g):
        rows = pl.ds(g * part, part)
        return swap(2 * PARTS + g, cross.at[1, rows, :], far_cols.at[rows, :])

    def swap_below(g):
        rows = pl.ds(g * part, part)
        return swap(3 * PARTS + g, below.at[rows, :], far_below.at[rows, :])

    def put(ref, q, value):
        ref[..., q * 8 : q * 8 + 8, :] = value.reshape(ref.shape[:-2] + (8, BS))

    def to_sibling(n, ref, got):
        return pltpu.make_async_remote_copy(
            src_ref=ref.at[1 - k], dst_ref=got,
            send_sem=core_send.at[n], recv_sem=core_recv.at[n],
            device_id=device(x, y, z, 1 - k), device_id_type=MESH,
        )

    def scatter_copy(g, got, land, o):
        px, py = chip_peer(o)
        return pltpu.make_async_remote_copy(
            src_ref=got.at[py, px], dst_ref=land.at[me],
            send_sem=rs_send.at[g, o], recv_sem=rs_recv.at[g, me],
            device_id=device(px, py, z, k), device_id_type=MESH,
        )

    def scatter_arrival(g, got, land, o):
        px, py = chip_peer(o)
        source = py * NX + px
        return pltpu.make_async_remote_copy(
            src_ref=got.at[py, px], dst_ref=land.at[source],
            send_sem=rs_send.at[g, o], recv_sem=rs_recv.at[g, source],
            device_id=device(px, py, z, k), device_id_type=MESH,
        )

    def scatter(g, encode, got, land):
        for row in range(NY):
            for col in range(NX):
                got[row, col] = encode(row, col)

        def send(o, carry):
            scatter_copy(g, got, land, o).start()
            return carry

        lax.fori_loop(0, CHIPS - 1, send, 0)
        land[me] = got[y, x]

    def collect(g, got, land):
        def take(o, carry):
            scatter_arrival(g, got, land, o).wait_recv()
            return carry

        lax.fori_loop(0, CHIPS - 1, take, 0)

    def y_copy(o, source):
        return pltpu.make_async_remote_copy(
            src_ref=k_own.at[(y + o) % NY], dst_ref=y_own.at[source],
            send_sem=y_send.at[o], recv_sem=y_recv.at[source],
            device_id=device(x, (y + o) % NY, z, k), device_id_type=MESH,
        )

    def row_copy(o, source):
        return pltpu.make_async_remote_copy(
            src_ref=s_own.at[(x + o) % NX], dst_ref=r_own.at[source],
            send_sem=row_send.at[o], recv_sem=row_recv.at[source],
            device_id=device((x + o) % NX, y, z, k), device_id_type=MESH,
        )

    def own_along_y():
        to_sibling(0, p_own, k_own).wait()
        for row in range(NY):
            k_own[row] = k_own[row] + p_own[k, row]
        for o in range(1, NY):
            y_copy(o, y).start()
        y_own[y] = k_own[y]

    def own_along_x():
        for o in range(1, NY):
            y_copy(o, (y + o) % NY).wait_recv()
        s_own[...] = (y_own[0] + y_own[1]) + (y_own[2] + y_own[3])
        for o in range(1, NX):
            row_copy(o, x).start()
        r_own[x] = s_own[x]

    load.wait()
    put(p_own, 0, gram(own[:, :BS], own[:, :BS]))
    put(p_own, 1, gram(own[:, :BS], own[:, BS:]))
    put(p_own, 2, gram(own[:, BS:], own[:, BS:]))
    to_sibling(0, p_own, k_own).start()

    per_part = CHUNKS // PARTS

    def pass_below(g):
        for j in range(g * per_part, (g + 1) * per_part):
            forward(j).wait_recv()
        swap_below(g).start()

    def take_rows(g):
        for j in range(g * per_part, (g + 1) * per_part):
            x_arrival(0, j).wait_recv()
        swap_rows(g, 0).start()
        swap_rows(g, 1).start()
        tokens = slice(g * part, (g + 1) * part)
        near = [cross[0, tokens, pl.ds(pl.multiple_of(i * BS + k * (BS // 2), BS // 2), BS // 2)] for i in range(2)]
        rows_t[:, tokens] = jnp.concatenate(near, axis=1).T

    for j in range(CHUNKS):
        x_arrival(1, j).wait_recv()
        forward(j).start()
        if j == 0:
            own_along_y()
        if (j + 1) % per_part == 0:
            g = j // per_part
            swap_cols(g).start()
            if g >= 1:
                take_rows(g - 1)
    take_rows(PARTS - 1)
    for g in range(PARTS - 2):
        pass_below(g)
    share_pairs.wait_recv()
    load_pairs.wait()
    far = pltpu.make_async_copy(pairs_far, pairs_all.at[1 - c], local_sem.at[2])
    far.start()

    for g in range(PARTS):
        swap_rows(g, 0).wait_recv()
        swap_rows(g, 1).wait_recv()
        rows_t[:, half + g * part : half + (g + 1) * part] = far_rows[g * part : (g + 1) * part, :].T
        swap_cols(g).wait_recv()

    def near_product(ref, first, last, cols):
        return jnp.dot(rows_t[:, first:last], ref[first:last, cols], preferred_element_type=jnp.float32)

    def far_product(ref, first, last, cols):
        return jnp.dot(
            rows_t[:, half + first : half + last], ref[first:last, cols], preferred_element_type=jnp.float32
        )

    def product(near, far_part, first, last, cols):
        return near_product(near, first, last, cols) + far_product(far_part, first, last, cols)

    def put_pairs(ref, j, both):
        put(ref, j, both[: BS // 2])
        put(ref, 2 + j, both[BS // 2 :])

    def peak(ref, q):
        top = None
        for row in range(NY):
            for col in range(NX):
                size = jnp.abs(ref[row, col, q * 8 : q * 8 + 8, :])
                top = size if top is None else jnp.maximum(top, size)
        return jnp.max(top, axis=0, keepdims=True)

    for j in range(2):
        put_pairs(p_mid, j, product(cross.at[1], far_cols, 0, half, slice(j * BS, (j + 1) * BS)))
    rows = [exponents(peak(p_mid, q)) for q in range(4)]
    scales[...] = jnp.zeros_like(scales)
    for q in range(4):
        scales[q : q + 1, :] = rows[q]
    grow[0:32, :] = spread([jnp.exp2(row * -0.125) for row in rows])
    scatter(0, lambda row, col: to_i16(compress(p_mid[row, col] * grow[0:32, :])), q_mid, r_mid)

    pass_below(PARTS - 2)
    edge.wait_recv()
    put(p_edge, 0, gram(own[:, BS:], ahead[...]))
    to_sibling(1, p_edge, k_edge).start()
    own_along_x()
    early = half - part
    for g in range(PARTS - 1):
        swap_below(g).wait_recv()
    for j in range(2):
        cols = slice(j * BS, (j + 1) * BS)
        sums_low[:, cols] = product(below, far_below, 0, early, cols)
    to_sibling(1, p_edge, k_edge).wait()
    k_edge[...] = k_edge[...] + p_edge[k]
    row = exponents(peak(k_edge, 0))
    scales[4:5, :] = row
    grow[32:40, :] = spread([jnp.exp2(row * -0.125)])

    def encode_edge(row, col):
        coded = compress(k_edge[row, col] * grow[32:40, :])
        return to_i16(jnp.concatenate([coded, scales[...]], axis=0))

    scatter(2, encode_edge, q_edge, r_edge)
    pass_below(PARTS - 1)
    for j in range(2):
        cols = slice(j * BS, (j + 1) * BS)
        sums_low[:, cols] = sums_low[:, cols] + near_product(below, early, half, cols)
    swap_below(PARTS - 1).wait_recv()
    for j in range(2):
        cols = slice(j * BS, (j + 1) * BS)
        put_pairs(p_low, j, sums_low[:, cols] + far_product(far_below, early, half, cols))
    rows = [exponents(jnp.maximum(peak(p_low, q), peak(p_low, 2 + q))) for q in range(2)]
    scales_low[...] = jnp.zeros_like(scales_low)
    for q in range(2):
        for h in range(2):
            scales_low[2 * q + h : 2 * q + h + 1, :] = rows[q][:, h * 128 : h * 128 + 128]
    grow[40:72, :] = spread([jnp.exp2(rows[q] * -0.125) for q in (0, 1, 0, 1)])

    def encode_low(row, col):
        coded = compress(p_low[row, col] * grow[40:72, :])
        return to_i16(jnp.concatenate([coded[:, :128], coded[:, 128:], scales_low[...]], axis=0))

    scatter(1, encode_low, q_low, r_low)

    far.wait()

    def code(reader, slot):
        row = pairs_all[reader, 0, 0, slot]
        col = pairs_all[reader, 1, 0, slot]
        at = (row - z * BAND) * WIDTH + col - row + BAND - 1
        return lookup[jnp.clip(at, 0, BAND * WIDTH - 1)]

    def note(o, carry):
        px, py, pk = plane_peer(o)
        slot = 2 * (((px % 2) * NY + py) * 2 + pk)
        for s in range(2):
            codes[2 * o + s] = code(px // 2, slot + s)
        return carry

    lax.fori_loop(0, 2 * CHIPS, note, 0)

    for o in range(1, NX):
        row_copy(o, (x + o) % NX).wait_recv()
    for side in range(2):
        table[3 * side : 3 * side + 3] = (r_own[2 * side] + r_own[2 * side + 1]).reshape(3, 8, BS)
    def pack(first, count):
        value = table[first : first + count]
        scale = exponents(jnp.max(jnp.abs(value), axis=2, keepdims=True))
        packed[first : first + count, :, :BS] = compress(value * jnp.exp2(scale * -0.125))
        packed[first : first + count, :, BS:] = jnp.broadcast_to(scale, (count, 8, 128))

    collect(2, q_edge, r_edge)
    edges = [None, None]
    for source in range(CHIPS):
        tail = to_f32(r_edge[source])
        factor[source] = jnp.exp2(tail[8:16, :] * 0.125)
        term = expand(tail[0:8, :]) * factor[source, 4:5, :]
        side = source % NX // 2
        edges[side] = term if edges[side] is None else edges[side] + term
    table[6] = edges[0]
    table[7] = edges[1]
    hop_up = pltpu.make_async_remote_copy(
        src_ref=table.at[pl.ds(6, 2)], dst_ref=table.at[pl.ds(20, 2)],
        send_sem=hop_send.at[0], recv_sem=hop_recv.at[0],
        device_id=device(x, y, up, k), device_id_type=MESH,
    )
    hop_up.start()
    collect(0, q_mid, r_mid)
    sums = None
    for source in range(CHIPS):
        term = expand(to_f32(r_mid[source])) * spread([factor[source, q : q + 1, :] for q in range(4)])
        sums = term if sums is None else sums + term
    table[8:12] = sums.reshape(4, 8, BS)
    pack(0, 12)

    collect(1, q_low, r_low)
    sums = [None, None]
    for source in range(CHIPS):
        coded = to_f32(r_low[source])
        scale = jnp.exp2(coded[64:80, :] * 0.125)
        for h in range(2):
            term = expand(coded[32 * h : 32 * h + 32, :]) * spread(
                [scale[2 * q + h : 2 * q + h + 1, :] for q in (0, 1, 0, 1)]
            )
            sums[h] = term if sums[h] is None else sums[h] + term
    table[12:16] = jnp.concatenate(sums, axis=1).reshape(4, 8, BS)
    hop_down = pltpu.make_async_remote_copy(
        src_ref=table.at[pl.ds(12, 4)], dst_ref=table.at[pl.ds(16, 4)],
        send_sem=hop_send.at[1], recv_sem=hop_recv.at[1],
        device_id=device(x, y, down, k), device_id_type=MESH,
    )
    hop_down.start()
    pack(12, 4)
    hop_up.wait()
    pack(20, 2)
    hop_down.wait()
    pack(16, 4)

    def fill(o):
        both = [packed[codes[2 * o + s] // 2] for s in range(2)]
        stage[o] = to_i16(jnp.concatenate(both, axis=0))

    rank = k * CHIPS + me

    def deliver(o):
        px, py, pk = plane_peer(o)
        return pltpu.make_async_remote_copy(
            src_ref=stage.at[o], dst_ref=arrived.at[rank],
            send_sem=out_send.at[o], recv_sem=out_recv.at[rank],
            device_id=device(px, py, z, pk), device_id_type=MESH,
        )

    def send_out(i, carry):
        for u in range(4):
            fill(4 * i + u)
        for u in range(4):
            deliver(4 * i + u).start()
        return carry

    groups = 2 * CHIPS // 4
    lax.fori_loop(0, groups - 1, send_out, 0)
    for u in range(4):
        fill(4 * (groups - 1) + u)
    for u in range(3):
        deliver(4 * (groups - 1) + u).start()
    arrived[rank] = stage[2 * CHIPS - 1]

    for j in range(CHUNKS):
        x_copy(0, j).wait_send()
        x_copy(1, j).wait_send()
        forward(j).wait_send()
    for g in range(PARTS):
        swap_rows(g, 0).wait_send()
        swap_rows(g, 1).wait_send()
        swap_cols(g).wait_send()
        swap_below(g).wait_send()
    for o in range(1, NY):
        y_copy(o, y).wait_send()
    for o in range(1, NX):
        row_copy(o, x).wait_send()
    edge.wait_send()
    share_pairs.wait_send()
    for g, got, land in ((0, q_mid, r_mid), (1, q_low, r_low), (2, q_edge, r_edge)):
        def left(o, carry):
            scatter_copy(g, got, land, o).wait_send()
            return carry

        lax.fori_loop(0, CHIPS - 1, left, 0)

    def left_out(o, carry):
        deliver(o).wait_send()
        return carry

    lax.fori_loop(0, 2 * CHIPS - 1, left_out, 0)

    def unpack(source):
        value = to_f32(arrived[source])
        scale = jnp.exp2(value[:, BS:] * 0.125)
        value = expand(value[:, :BS]) * jnp.concatenate([scale, scale], axis=1)
        blocks[0, source] = value[:8]
        blocks[1, source] = value[8:]

    def take_out(o, carry):
        px, py, pk = plane_peer(o)
        source = pk * CHIPS + py * NX + px
        pltpu.make_async_remote_copy(
            src_ref=stage.at[o], dst_ref=arrived.at[source],
            send_sem=out_send.at[o], recv_sem=out_recv.at[source],
            device_id=device(px, py, z, pk), device_id_type=MESH,
        ).wait_recv()
        return carry

    lax.fori_loop(0, 2 * CHIPS - 1, take_out, 0)

    def unpack_four(i, carry):
        for u in range(4):
            unpack(4 * i + u)
        return carry

    lax.fori_loop(0, groups, unpack_four, 0)
    for s in range(2):
        slot = 2 * token + s
        block = blocks[s].reshape(BS, BS)
        flip = code(c, slot) % 2 == 1
        block = jnp.where(flip, block.T, block)
        out_ref[0, s] = jnp.where(slot < counts_ref[0], block * weight, 0.0)


def shards(layer_input, pairs, counts):
    rows, columns = layer_input.shape
    weight = 2.0 / (rows * lax.axis_size("token"))
    dma, vmem = pltpu.SemaphoreType.DMA, pltpu.VMEM
    f32, bf16, i16 = jnp.float32, jnp.bfloat16, jnp.int16
    slots = pairs.shape[2] // lax.axis_size("token")
    scratch = [
        vmem((rows, columns), bf16),
        vmem((2, rows // 2, columns), bf16),
        vmem((rows // 2, columns), bf16),
        vmem((rows, BS), bf16),
    ]
    scratch += [
        vmem((rows // 2, BS), bf16),
        vmem((rows // 2, columns), bf16),
        vmem((rows // 2, columns), bf16),
        vmem((2, NY, NX, 24, BS), f32), vmem((NY, NX, 24, BS), f32),
        vmem((BS, rows), bf16), vmem((BS, columns), f32),
        vmem((NY, NX, 32, BS), f32), vmem((NY, NX, 32, BS), f32),
        vmem((2, NY, NX, 8, BS), f32), vmem((NY, NX, 8, BS), f32),
        vmem((NY, NX, 32, BS), i16), vmem((NY, NX, 80, 128), i16), vmem((NY, NX, 16, BS), i16),
        vmem((8, BS), f32), vmem((16, 128), f32), vmem((NX, 24, BS), f32),
        vmem((CHIPS, 32, BS), i16), vmem((CHIPS, 80, 128), i16), vmem((CHIPS, 16, BS), i16),
        vmem((72, BS), f32), vmem((CHIPS, 8, BS), f32),
    ]
    scratch += [
        vmem((22, 8, BS), f32),
        vmem((22, 8, BS + 128), f32),
        vmem((slots, 2 * CHIPS, 8, BS), f32),
        vmem((2 * CHIPS, 8 * slots, BS + 128), i16),
        vmem((2 * CHIPS, 8 * slots, BS + 128), i16),
        vmem(pairs.shape, jnp.int32),
        pltpu.SMEM((2,) + pairs.shape, jnp.int32),
        pltpu.SMEM((BAND * WIDTH,), jnp.int32),
        pltpu.SMEM((4 * CHIPS,), jnp.int32),
        dma((3,)),
        dma((2, CHUNKS)), dma((2, CHUNKS)),
        dma((CHUNKS,)), dma((CHUNKS,)),
        dma, dma, dma, dma,
        dma((2,)), dma((2,)), dma((4 * PARTS,)), dma((4 * PARTS,)),
        vmem((NY, NX, 24, BS), f32), vmem((NX, 24, BS), f32),
        dma((NY,)), dma((NY,)), dma((NX,)), dma((NX,)),
        dma((3, CHIPS)), dma((3, CHIPS)),
        dma((2,)), dma((2,)),
        dma((2 * CHIPS,)), dma((2 * CHIPS,)),
    ]
    return pl.pallas_call(
        functools.partial(kernel, weight),
        out_shape=jax.ShapeDtypeStruct((1, slots, BS, BS), f32),
        in_specs=[
            pl.BlockSpec(memory_space=pltpu.HBM),
            pl.BlockSpec(memory_space=pltpu.HBM),
            pl.BlockSpec(memory_space=pltpu.SMEM),
        ],
        out_specs=pl.BlockSpec(memory_space=pltpu.VMEM),
        scratch_shapes=scratch,
        compiler_params=pltpu.CompilerParams(
            collective_id=0, has_side_effects=True, vmem_limit_bytes=211 * 2**18
        ),
    )(layer_input, pairs, counts)


def solution(mesh):
    return jax.shard_map(
        shards,
        mesh=mesh,
        in_specs=(
            P("token", ("brow", "bcol")),
            P(None, ("brow", "bcol"), None),
            P(("brow", "bcol")),
        ),
        out_specs=P(("brow", "bcol"), "token", None, None),
        check_vma=False,
    )
```

```python
import functools
import jax
import jax.numpy as jnp
from jax import lax
from jax.experimental import pallas as pl
from jax.experimental.pallas import tpu as pltpu
from jax.sharding import PartitionSpec as P

BS = 256
BAND = 4
NX, NY, NZ = 4, 4, 8
CHIPS = NX * NY
CHUNKS = 8
PARTS = 4
FULL = 32000.0
MESH = pl.DeviceIdType.MESH

TABLE = {
    (0, 0): (0, 0), (0, 1): (1, 0), (1, 1): (2, 0),
    (2, 2): (3, 0), (2, 3): (4, 0), (3, 3): (5, 0),
    (1, 4): (6, 0), (3, 6): (7, 0),
    (0, 2): (8, 0), (0, 3): (9, 0), (1, 2): (10, 0), (1, 3): (11, 0),
    (0, -2): (12, 0), (0, -1): (13, 0), (1, -2): (14, 0), (1, -1): (15, 0),
    (2, 4): (16, 1), (3, 4): (17, 1), (2, 5): (18, 1), (3, 5): (19, 1),
    (0, -3): (20, 1), (2, -1): (21, 1),
    (1, 0): (1, 1), (3, 2): (4, 1),
    (2, 0): (8, 1), (3, 0): (9, 1), (2, 1): (10, 1), (3, 1): (11, 1),
}
WIDTH = 2 * BAND - 1


def device(x, y, z, k):
    return (((x % 2) * NY + y) * 2 + k, z, x // 2)


def gram(a, b):
    return lax.dot_general(a, b, (((0,), (0,)), ((), ())), preferred_element_type=jnp.float32)


def far_first(n):
    return (2 + 3 * n + 3 * (n * (n - 1) // 2)) % 4


def exponents(peak):
    return jnp.ceil(8.0 * jnp.log2(jnp.maximum(peak, 1e-30)))


def spread(rows):
    return jnp.concatenate([jnp.broadcast_to(row, (8, row.shape[1])) for row in rows], axis=0)


def compress(value):
    root = FULL * jnp.sqrt(jnp.abs(value))
    return jnp.where(value < 0.0, -root, root)


def expand(coded):
    return coded * jnp.abs(coded) * (1.0 / (FULL * FULL))


def to_i16(value):
    return jnp.floor(value + 0.5).astype(jnp.int32).astype(jnp.int16)


def to_f32(value):
    return value.astype(jnp.int32).astype(jnp.float32)


def kernel(
    weight, x_ref, pairs_ref, counts_ref, out_ref,
    own, cross, below, ahead, far_rows, far_cols, far_below,
    p_own, k_own, rows_t, sums_low, p_mid, p_low, p_edge, k_edge, q_mid, q_low, q_edge, scales, scales_low, r_own, r_mid, r_low, r_edge, grow, factor, table, packed, blocks, stage, arrived, pairs_far, pairs_all, lookup, codes,
    local_sem, x_send, x_recv, zf_send, zf_recv, ze_send, ze_recv, pr_send, pr_recv,
    core_send, core_recv, swap_send, swap_recv, y_own, s_own, y_send, y_recv, row_send, row_recv, rs_send, rs_recv, hop_send, hop_recv, out_send, out_recv,
):
    token = lax.axis_index("token")
    z = lax.axis_index("brow")
    c = lax.axis_index("bcol")
    k = token % 2
    y = (token // 2) % NY
    x = 2 * c + token // (2 * NY)
    me = y * NX + x
    half = x_ref.shape[0] // 2
    step = half // CHUNKS
    up, down = (z + 1) % NZ, (z + NZ - 1) % NZ

    load = pltpu.make_async_copy(x_ref, own, local_sem.at[0])
    load.start()
    load_pairs = pltpu.make_async_copy(pairs_ref, pairs_all.at[c], local_sem.at[1])
    load_pairs.start()

    barrier = pltpu.get_barrier_semaphore()

    def chip_peer(o):
        return (x + far_first(o % NX)) % NX, (y + far_first(o // NX)) % NY

    def plane_peer(o):
        return chip_peer(o // 2) + ((k + 1 - o % 2) % 2,)

    near = [device((x + o) % NX, y, z, k) for o in (2, 1, 3)]
    near += [device(x, (y + o) % NY, z, k) for o in (2, 1, 3)]
    near += [device(x, y, up, k), device(x, y, down, k), device(x, y, z, 1 - k)]
    for peer in near:
        pl.semaphore_signal(barrier, inc=1, device_id=peer, device_id_type=MESH)
    for (row, col), (at, flip) in TABLE.items():
        lookup[row * WIDTH + col - row + BAND - 1] = at * 2 + flip
    pl.semaphore_wait(barrier, len(near))

    def x_copy(direction, j):
        to = device((x + 1) % NX, y, z, k) if direction == 0 else device((x + NX - 1) % NX, y, z, k)
        first = (c if direction == 0 else 1 - c) * half + j * step
        return pltpu.make_async_remote_copy(
            src_ref=x_ref.at[pl.ds(first, step), :],
            dst_ref=cross.at[c, pl.ds(j * step, step), :],
            send_sem=x_send.at[direction, j],
            recv_sem=x_recv.at[c, j],
            device_id=to, device_id_type=MESH,
        )

    def x_arrival(side, j):
        return pltpu.make_async_remote_copy(
            src_ref=x_ref.at[pl.ds(0, step), :],
            dst_ref=cross.at[side, pl.ds(j * step, step), :],
            send_sem=x_send.at[0, j],
            recv_sem=x_recv.at[side, j],
            device_id=device((x + 1) % NX, y, z, k), device_id_type=MESH,
        )

    def forward(j):
        return pltpu.make_async_remote_copy(
            src_ref=cross.at[1, pl.ds(j * step, step), :],
            dst_ref=below.at[pl.ds(j * step, step), :],
            send_sem=zf_send.at[j], recv_sem=zf_recv.at[j],
            device_id=device(x, y, up, k), device_id_type=MESH,
        )

    for j in range(CHUNKS):
        x_copy(0, j).start()
        x_copy(1, j).start()
    edge = pltpu.make_async_remote_copy(
        src_ref=x_ref.at[:, pl.ds(0, BS)], dst_ref=ahead,
        send_sem=ze_send, recv_sem=ze_recv,
        device_id=device(x, y, down, k), device_id_type=MESH,
    )
    edge.start()
    share_pairs = pltpu.make_async_remote_copy(
        src_ref=pairs_ref, dst_ref=pairs_far, send_sem=pr_send, recv_sem=pr_recv,
        device_id=device((x + 2) % NX, y, z, k), device_id_type=MESH,
    )
    share_pairs.start()

    def swap(n, source, target):
        return pltpu.make_async_remote_copy(
            src_ref=source, dst_ref=target,
            send_sem=swap_send.at[n], recv_sem=swap_recv.at[n],
            device_id=device(x, y, z, 1 - k), device_id_type=MESH,
        )

    part = half // PARTS

    def swap_rows(g, i):
        rows = pl.ds(g * part, part)
        first = pl.multiple_of(i * BS + (1 - k) * (BS // 2), BS // 2)
        return swap(
            2 * g + i, cross.at[0, rows, pl.ds(first, BS // 2)],
            far_rows.at[rows, i * (BS // 2) : (i + 1) * (BS // 2)],
        )

    def swap_cols(g):
        rows = pl.ds(g * part, part)
        return swap(2 * PARTS + g, cross.at[1, rows, :], far_cols.at[rows, :])

    def swap_below(g):
        rows = pl.ds(g * part, part)
        return swap(3 * PARTS + g, below.at[rows, :], far_below.at[rows, :])

    def put(ref, q, value):
        ref[..., q * 8 : q * 8 + 8, :] = value.reshape(ref.shape[:-2] + (8, BS))

    def to_sibling(n, ref, got):
        return pltpu.make_async_remote_copy(
            src_ref=ref.at[1 - k], dst_ref=got,
            send_sem=core_send.at[n], recv_sem=core_recv.at[n],
            device_id=device(x, y, z, 1 - k), device_id_type=MESH,
        )

    def scatter_copy(g, got, land, o):
        px, py = chip_peer(o)
        return pltpu.make_async_remote_copy(
            src_ref=got.at[py, px], dst_ref=land.at[me],
            send_sem=rs_send.at[g, o], recv_sem=rs_recv.at[g, me],
            device_id=device(px, py, z, k), device_id_type=MESH,
        )

    def scatter_arrival(g, got, land, o):
        px, py = chip_peer(o)
        source = py * NX + px
        return pltpu.make_async_remote_copy(
            src_ref=got.at[py, px], dst_ref=land.at[source],
            send_sem=rs_send.at[g, o], recv_sem=rs_recv.at[g, source],
            device_id=device(px, py, z, k), device_id_type=MESH,
        )

    def scatter(g, encode, got, land):
        for row in range(NY):
            for col in range(NX):
                got[row, col] = encode(row, col)

        def send(o, carry):
            scatter_copy(g, got, land, o).start()
            return carry

        lax.fori_loop(0, CHIPS - 1, send, 0)
        land[me] = got[y, x]

    def collect(g, got, land):
        def take(o, carry):
            scatter_arrival(g, got, land, o).wait_recv()
            return carry

        lax.fori_loop(0, CHIPS - 1, take, 0)

    def y_copy(o, source):
        return pltpu.make_async_remote_copy(
            src_ref=k_own.at[(y + o) % NY], dst_ref=y_own.at[source],
            send_sem=y_send.at[o], recv_sem=y_recv.at[source],
            device_id=device(x, (y + o) % NY, z, k), device_id_type=MESH,
        )

    def row_copy(o, source):
        return pltpu.make_async_remote_copy(
            src_ref=s_own.at[(x + o) % NX], dst_ref=r_own.at[source],
            send_sem=row_send.at[o], recv_sem=row_recv.at[source],
            device_id=device((x + o) % NX, y, z, k), device_id_type=MESH,
        )

    def own_along_y():
        to_sibling(0, p_own, k_own).wait()
        for row in range(NY):
            k_own[row] = k_own[row] + p_own[k, row]
        for o in range(1, NY):
            y_copy(o, y).start()
        y_own[y] = k_own[y]

    def own_along_x():
        for o in range(1, NY):
            y_copy(o, (y + o) % NY).wait_recv()
        s_own[...] = (y_own[0] + y_own[1]) + (y_own[2] + y_own[3])
        for o in range(1, NX):
            row_copy(o, x).start()
        r_own[x] = s_own[x]

    load.wait()
    put(p_own, 0, gram(own[:, :BS], own[:, :BS]))
    put(p_own, 1, gram(own[:, :BS], own[:, BS:]))
    put(p_own, 2, gram(own[:, BS:], own[:, BS:]))
    to_sibling(0, p_own, k_own).start()

    per_part = CHUNKS // PARTS

    def pass_below(g):
        for j in range(g * per_part, (g + 1) * per_part):
            forward(j).wait_recv()
        swap_below(g).start()

    def take_rows(g):
        for j in range(g * per_part, (g + 1) * per_part):
            x_arrival(0, j).wait_recv()
        swap_rows(g, 0).start()
        swap_rows(g, 1).start()
        tokens = slice(g * part, (g + 1) * part)
        near = [cross[0, tokens, pl.ds(pl.multiple_of(i * BS + k * (BS // 2), BS // 2), BS // 2)] for i in range(2)]
        rows_t[:, tokens] = jnp.concatenate(near, axis=1).T

    for j in range(CHUNKS):
        x_arrival(1, j).wait_recv()
        forward(j).start()
        if j == 0:
            own_along_y()
        if (j + 1) % per_part == 0:
            g = j // per_part
            swap_cols(g).start()
            if g >= 1:
                take_rows(g - 1)
    take_rows(PARTS - 1)
    for g in range(PARTS - 2):
        pass_below(g)
    share_pairs.wait_recv()
    load_pairs.wait()
    far = pltpu.make_async_copy(pairs_far, pairs_all.at[1 - c], local_sem.at[2])
    far.start()

    for g in range(PARTS):
        swap_rows(g, 0).wait_recv()
        swap_rows(g, 1).wait_recv()
        rows_t[:, half + g * part : half + (g + 1) * part] = far_rows[g * part : (g + 1) * part, :].T
        swap_cols(g).wait_recv()

    def near_product(ref, first, last, cols):
        return jnp.dot(rows_t[:, first:last], ref[first:last, cols], preferred_element_type=jnp.float32)

    def far_product(ref, first, last, cols):
        return jnp.dot(
            rows_t[:, half + first : half + last], ref[first:last, cols], preferred_element_type=jnp.float32
        )

    def product(near, far_part, first, last, cols):
        return near_product(near, first, last, cols) + far_product(far_part, first, last, cols)

    def put_pairs(ref, j, both):
        put(ref, j, both[: BS // 2])
        put(ref, 2 + j, both[BS // 2 :])

    def peak(ref, q):
        top = None
        for row in range(NY):
            for col in range(NX):
                size = jnp.abs(ref[row, col, q * 8 : q * 8 + 8, :])
                top = size if top is None else jnp.maximum(top, size)
        return jnp.max(top, axis=0, keepdims=True)

    for j in range(2):
        put_pairs(p_mid, j, product(cross.at[1], far_cols, 0, half, slice(j * BS, (j + 1) * BS)))
    rows = [exponents(peak(p_mid, q)) for q in range(4)]
    scales[...] = jnp.zeros_like(scales)
    for q in range(4):
        scales[q : q + 1, :] = rows[q]
    grow[0:32, :] = spread([jnp.exp2(row * -0.125) for row in rows])
    scatter(0, lambda row, col: to_i16(compress(p_mid[row, col] * grow[0:32, :])), q_mid, r_mid)

    pass_below(PARTS - 2)
    edge.wait_recv()
    put(p_edge, 0, gram(own[:, BS:], ahead[...]))
    to_sibling(1, p_edge, k_edge).start()
    own_along_x()
    early = half - part
    for g in range(PARTS - 1):
        swap_below(g).wait_recv()
    for j in range(2):
        cols = slice(j * BS, (j + 1) * BS)
        sums_low[:, cols] = product(below, far_below, 0, early, cols)
    to_sibling(1, p_edge, k_edge).wait()
    k_edge[...] = k_edge[...] + p_edge[k]
    row = exponents(peak(k_edge, 0))
    scales[4:5, :] = row
    grow[32:40, :] = spread([jnp.exp2(row * -0.125)])

    def encode_edge(row, col):
        coded = compress(k_edge[row, col] * grow[32:40, :])
        return to_i16(jnp.concatenate([coded, scales[...]], axis=0))

    scatter(2, encode_edge, q_edge, r_edge)
    pass_below(PARTS - 1)
    for j in range(2):
        cols = slice(j * BS, (j + 1) * BS)
        sums_low[:, cols] = sums_low[:, cols] + near_product(below, early, half, cols)
    swap_below(PARTS - 1).wait_recv()
    for j in range(2):
        cols = slice(j * BS, (j + 1) * BS)
        put_pairs(p_low, j, sums_low[:, cols] + far_product(far_below, early, half, cols))
    rows = [exponents(jnp.maximum(peak(p_low, q), peak(p_low, 2 + q))) for q in range(2)]
    scales_low[...] = jnp.zeros_like(scales_low)
    for q in range(2):
        for h in range(2):
            scales_low[2 * q + h : 2 * q + h + 1, :] = rows[q][:, h * 128 : h * 128 + 128]
    grow[40:72, :] = spread([jnp.exp2(rows[q] * -0.125) for q in (0, 1, 0, 1)])

    def encode_low(row, col):
        coded = compress(p_low[row, col] * grow[40:72, :])
        return to_i16(jnp.concatenate([coded[:, :128], coded[:, 128:], scales_low[...]], axis=0))

    scatter(1, encode_low, q_low, r_low)

    far.wait()

    def code(reader, slot):
        row = pairs_all[reader, 0, 0, slot]
        col = pairs_all[reader, 1, 0, slot]
        at = (row - z * BAND) * WIDTH + col - row + BAND - 1
        return lookup[jnp.clip(at, 0, BAND * WIDTH - 1)]

    def note(o, carry):
        px, py, pk = plane_peer(o)
        slot = 2 * (((px % 2) * NY + py) * 2 + pk)
        for s in range(2):
            codes[2 * o + s] = code(px // 2, slot + s)
        return carry

    lax.fori_loop(0, 2 * CHIPS, note, 0)

    for o in range(1, NX):
        row_copy(o, (x + o) % NX).wait_recv()
    for side in range(2):
        table[3 * side : 3 * side + 3] = (r_own[2 * side] + r_own[2 * side + 1]).reshape(3, 8, BS)
    def pack(first, count):
        value = table[first : first + count]
        scale = exponents(jnp.max(jnp.abs(value), axis=2, keepdims=True))
        packed[first : first + count, :, :BS] = compress(value * jnp.exp2(scale * -0.125))
        packed[first : first + count, :, BS:] = jnp.broadcast_to(scale, (count, 8, 128))

    collect(2, q_edge, r_edge)
    edges = [None, None]
    for source in range(CHIPS):
        tail = to_f32(r_edge[source])
        factor[source] = jnp.exp2(tail[8:16, :] * 0.125)
        term = expand(tail[0:8, :]) * factor[source, 4:5, :]
        side = source % NX // 2
        edges[side] = term if edges[side] is None else edges[side] + term
    table[6] = edges[0]
    table[7] = edges[1]
    hop_up = pltpu.make_async_remote_copy(
        src_ref=table.at[pl.ds(6, 2)], dst_ref=table.at[pl.ds(20, 2)],
        send_sem=hop_send.at[0], recv_sem=hop_recv.at[0],
        device_id=device(x, y, up, k), device_id_type=MESH,
    )
    hop_up.start()
    collect(0, q_mid, r_mid)
    sums = None
    for source in range(CHIPS):
        term = expand(to_f32(r_mid[source])) * spread([factor[source, q : q + 1, :] for q in range(4)])
        sums = term if sums is None else sums + term
    table[8:12] = sums.reshape(4, 8, BS)
    pack(0, 12)

    collect(1, q_low, r_low)
    sums = [None, None]
    for source in range(CHIPS):
        coded = to_f32(r_low[source])
        scale = jnp.exp2(coded[64:80, :] * 0.125)
        for h in range(2):
            term = expand(coded[32 * h : 32 * h + 32, :]) * spread(
                [scale[2 * q + h : 2 * q + h + 1, :] for q in (0, 1, 0, 1)]
            )
            sums[h] = term if sums[h] is None else sums[h] + term
    table[12:16] = jnp.concatenate(sums, axis=1).reshape(4, 8, BS)
    hop_down = pltpu.make_async_remote_copy(
        src_ref=table.at[pl.ds(12, 4)], dst_ref=table.at[pl.ds(16, 4)],
        send_sem=hop_send.at[1], recv_sem=hop_recv.at[1],
        device_id=device(x, y, down, k), device_id_type=MESH,
    )
    hop_down.start()
    pack(12, 4)
    hop_up.wait()
    pack(20, 2)
    hop_down.wait()
    pack(16, 4)

    def fill(o):
        both = [packed[codes[2 * o + s] // 2] for s in range(2)]
        stage[o] = to_i16(jnp.concatenate(both, axis=0))

    rank = k * CHIPS + me

    def deliver(o):
        px, py, pk = plane_peer(o)
        return pltpu.make_async_remote_copy(
            src_ref=stage.at[o], dst_ref=arrived.at[rank],
            send_sem=out_send.at[o], recv_sem=out_recv.at[rank],
            device_id=device(px, py, z, pk), device_id_type=MESH,
        )

    def send_out(i, carry):
        for u in range(2):
            fill(2 * i + u)
        for u in range(2):
            deliver(2 * i + u).start()
        return carry

    groups = 2 * CHIPS // 4
    lax.fori_loop(0, CHIPS - 1, send_out, 0)
    fill(2 * CHIPS - 2)
    deliver(2 * CHIPS - 2).start()
    fill(2 * CHIPS - 1)
    arrived[rank] = stage[2 * CHIPS - 1]

    for j in range(CHUNKS):
        x_copy(0, j).wait_send()
        x_copy(1, j).wait_send()
        forward(j).wait_send()
    for g in range(PARTS):
        swap_rows(g, 0).wait_send()
        swap_rows(g, 1).wait_send()
        swap_cols(g).wait_send()
        swap_below(g).wait_send()
    for o in range(1, NY):
        y_copy(o, y).wait_send()
    for o in range(1, NX):
        row_copy(o, x).wait_send()
    edge.wait_send()
    share_pairs.wait_send()
    for g, got, land in ((0, q_mid, r_mid), (1, q_low, r_low), (2, q_edge, r_edge)):
        def left(o, carry):
            scatter_copy(g, got, land, o).wait_send()
            return carry

        lax.fori_loop(0, CHIPS - 1, left, 0)

    def left_out(o, carry):
        deliver(o).wait_send()
        return carry

    lax.fori_loop(0, 2 * CHIPS - 1, left_out, 0)

    def unpack(source):
        value = to_f32(arrived[source])
        scale = jnp.exp2(value[:, BS:] * 0.125)
        value = expand(value[:, :BS]) * jnp.concatenate([scale, scale], axis=1)
        blocks[0, source] = value[:8]
        blocks[1, source] = value[8:]

    def take_out(o, carry):
        px, py, pk = plane_peer(o)
        source = pk * CHIPS + py * NX + px
        pltpu.make_async_remote_copy(
            src_ref=stage.at[o], dst_ref=arrived.at[source],
            send_sem=out_send.at[o], recv_sem=out_recv.at[source],
            device_id=device(px, py, z, pk), device_id_type=MESH,
        ).wait_recv()
        return carry

    lax.fori_loop(0, 2 * CHIPS - 1, take_out, 0)

    def unpack_four(i, carry):
        for u in range(4):
            unpack(4 * i + u)
        return carry

    lax.fori_loop(0, groups, unpack_four, 0)
    for s in range(2):
        slot = 2 * token + s
        block = blocks[s].reshape(BS, BS)
        flip = code(c, slot) % 2 == 1
        block = jnp.where(flip, block.T, block)
        out_ref[0, s] = jnp.where(slot < counts_ref[0], block * weight, 0.0)


def shards(layer_input, pairs, counts):
    rows, columns = layer_input.shape
    weight = 2.0 / (rows * lax.axis_size("token"))
    dma, vmem = pltpu.SemaphoreType.DMA, pltpu.VMEM
    f32, bf16, i16 = jnp.float32, jnp.bfloat16, jnp.int16
    slots = pairs.shape[2] // lax.axis_size("token")
    scratch = [
        vmem((rows, columns), bf16),
        vmem((2, rows // 2, columns), bf16),
        vmem((rows // 2, columns), bf16),
        vmem((rows, BS), bf16),
    ]
    scratch += [
        vmem((rows // 2, BS), bf16),
        vmem((rows // 2, columns), bf16),
        vmem((rows // 2, columns), bf16),
        vmem((2, NY, NX, 24, BS), f32), vmem((NY, NX, 24, BS), f32),
        vmem((BS, rows), bf16), vmem((BS, columns), f32),
        vmem((NY, NX, 32, BS), f32), vmem((NY, NX, 32, BS), f32),
        vmem((2, NY, NX, 8, BS), f32), vmem((NY, NX, 8, BS), f32),
        vmem((NY, NX, 32, BS), i16), vmem((NY, NX, 80, 128), i16), vmem((NY, NX, 16, BS), i16),
        vmem((8, BS), f32), vmem((16, 128), f32), vmem((NX, 24, BS), f32),
        vmem((CHIPS, 32, BS), i16), vmem((CHIPS, 80, 128), i16), vmem((CHIPS, 16, BS), i16),
        vmem((72, BS), f32), vmem((CHIPS, 8, BS), f32),
    ]
    scratch += [
        vmem((22, 8, BS), f32),
        vmem((22, 8, BS + 128), f32),
        vmem((slots, 2 * CHIPS, 8, BS), f32),
        vmem((2 * CHIPS, 8 * slots, BS + 128), i16),
        vmem((2 * CHIPS, 8 * slots, BS + 128), i16),
        vmem(pairs.shape, jnp.int32),
        pltpu.SMEM((2,) + pairs.shape, jnp.int32),
        pltpu.SMEM((BAND * WIDTH,), jnp.int32),
        pltpu.SMEM((4 * CHIPS,), jnp.int32),
        dma((3,)),
        dma((2, CHUNKS)), dma((2, CHUNKS)),
        dma((CHUNKS,)), dma((CHUNKS,)),
        dma, dma, dma, dma,
        dma((2,)), dma((2,)), dma((4 * PARTS,)), dma((4 * PARTS,)),
        vmem((NY, NX, 24, BS), f32), vmem((NX, 24, BS), f32),
        dma((NY,)), dma((NY,)), dma((NX,)), dma((NX,)),
        dma((3, CHIPS)), dma((3, CHIPS)),
        dma((2,)), dma((2,)),
        dma((2 * CHIPS,)), dma((2 * CHIPS,)),
    ]
    return pl.pallas_call(
        functools.partial(kernel, weight),
        out_shape=jax.ShapeDtypeStruct((1, slots, BS, BS), f32),
        in_specs=[
            pl.BlockSpec(memory_space=pltpu.HBM),
            pl.BlockSpec(memory_space=pltpu.HBM),
            pl.BlockSpec(memory_space=pltpu.SMEM),
        ],
        out_specs=pl.BlockSpec(memory_space=pltpu.VMEM),
        scratch_shapes=scratch,
        compiler_params=pltpu.CompilerParams(
            collective_id=0, has_side_effects=True, vmem_limit_bytes=211 * 2**18
        ),
    )(layer_input, pairs, counts)


def solution(mesh):
    return jax.shard_map(
        shards,
        mesh=mesh,
        in_specs=(
            P("token", ("brow", "bcol")),
            P(None, ("brow", "bcol"), None),
            P(("brow", "bcol")),
        ),
        out_specs=P(("brow", "bcol"), "token", None, None),
        check_vma=False,
    )
```
